128 devices in a mesh: context: 32 (over y, z, core), tensor: 4 (over x).
Axes of the slice: x: 4, y: 4, z: 4, core: 2. Of those that a mesh axis runs over, the one named last changes fastest.
Arguments:
- mixer_input: bfloat16 [8192, 8192], P('context', 'tensor'), may hold values from -6 to 6
- step_raw: float32 [8192, 128], P('context', 'tensor'), may hold values from -3 to 3
- step_bias: float32 [128], P('tensor'), may hold values from -1 to 0.5
- decay_log: float32 [128], P('tensor'), may hold values from -14 to -3
- skip_gain: float32 [128], P('tensor'), may hold values from 0.5 to 1.5
- write_keys: bfloat16 [8192, 1024], P('context', 'tensor'), may hold values from -0.125 to 0.125
- read_keys: bfloat16 [8192, 1024], P('context', 'tensor'), may hold values from -0.375 to 0.375
- document_ids: int32 [8192], P('context'), may hold values from 0 to 2, never falling along the last dimension, each value on 1 to 4096 neighbouring positions
- query_rows: bfloat16 [8192, 4096], P('context', 'tensor'), may hold values from -128 to 128
- key_rows: bfloat16 [8192, 512], P(('context', 'tensor')), may hold values from -6 to 6
- value_rows: bfloat16 [8192, 512], P(('context', 'tensor')), may hold values from -6 to 6
Outputs:
- mixer_output: bfloat16 [8192, 8192], P('context', 'tensor')
- attention_output: bfloat16 [8192, 4096], P('context', 'tensor')
The draws below stay inside these ranges and needn't reach their ends.
Inputs may be any that keep to these rules, and one draw needn't show every extreme that they name: `document_ids`: never falling along the sequence; one document holds exactly 4096 tokens.
All inputs are finite; a program needn't handle non-finite values.
Results may differ from the reference program's by a relative error of at most 0.011.
Values may be sent and summed in bfloat16 or wider, within the bound.
No kernel may reach another device: no remote copies, remote signals or barrier semaphores. Data moves between devices by JAX's collectives and lax.ppermute only.
A program may use at most 192 MiB of HBM per device.

```python
import math
from functools import partial
import jax
import jax.numpy as jnp
import numpy as np
from jax import lax

TOK_DEV = 256
HEADS = 128
HEAD_DIM = 64
DSTATE = 256
GROUPS = 4
QHEADS = 32
KVHEADS = 4
ATT_DIM = 128
DOCS = 3
SEQ = 8192


def shared_rows(key):
    normal_key = jax.random.fold_in(key, 1)
    normals = jnp.clip(jax.random.normal(normal_key, (SEQ, KVHEADS * ATT_DIM), jnp.float32), -3.3, 3.3)
    basis = normals
    row_index = jnp.arange(SEQ)
    marked = (row_index % TOK_DEV == TOK_DEV - 2)[:, None]
    return jnp.where(marked, basis, basis)


def draw_key_rows(key, part):
    table = shared_rows(key)
    return table.astype(jnp.bfloat16)


def draw_query_rows(key, part):
    key = jax.random.fold_in(key, 7)
    basis = jnp.clip(2.5 * jax.random.normal(key, (SEQ, QHEADS * ATT_DIM), jnp.float32), -16.0, 16.0)
    row_index = jnp.arange(SEQ)
    marked = (row_index % TOK_DEV == TOK_DEV - 1)[:, None]
    return jnp.where(marked, basis, basis).astype(jnp.bfloat16)


def draw_step_raw(key, part):
    key = jax.random.fold_in(key, 3)
    first_key, second_key = jax.random.split(key)
    offsets = jnp.repeat(jax.random.uniform(first_key, (SEQ // TOK_DEV, 1), jnp.float32, -1.2, 1.2), TOK_DEV, axis=0)
    noise = 0.5 * jnp.clip(jax.random.normal(second_key, (SEQ, HEADS), jnp.float32), -3.5, 3.5)
    return offsets + noise


def draw_decay_log(key, part):
    key = jax.random.fold_in(key, 5)
    pick_key, slow_key, quick_key, middle_key = jax.random.split(key, 4)
    quick_share = 2
    middle_share = 5
    picked = jax.random.randint(pick_key, (HEADS,), 0, 10)
    slow_rate = jnp.exp(jax.random.uniform(slow_key, (HEADS,), jnp.float32, jnp.log(0.2), jnp.log(1.5))) / SEQ
    quick_rate = jnp.exp(jax.random.uniform(quick_key, (HEADS,), jnp.float32, jnp.log(1.0 / 50.0), jnp.log(1.0 / 30.0))) / 0.75
    middle_rate = jnp.exp(jax.random.uniform(middle_key, (HEADS,), jnp.float32, jnp.log(1.0 / 2000.0), jnp.log(1.0 / 300.0)))
    rates = jnp.where(picked < quick_share, quick_rate, jnp.where(picked < middle_share, middle_rate, slow_rate))
    return jnp.log(rates)


def steps_of(stream_key, extent, cuts, least, high):
    factor_of, own = 1.0, jax.random.fold_in(stream_key, 6)
    for axis_at, blocks in cuts:
        draws = jnp.exp(jax.random.uniform(jax.random.fold_in(own, axis_at), (blocks,), jnp.float32, least / len(cuts), high / len(cuts)))
        factor_of = factor_of * jnp.repeat(draws, extent[axis_at] // blocks).reshape([-1 if axis == axis_at else 1 for axis in range(len(extent))])
    return factor_of


def split_up(count, total, most, slope):
    portions = [(1 << 20) // math.isqrt(rank ** slope) + 1 for rank in range(2, count + 1)]
    rest, counts = total - most - (count - 1), [1] * (count - 1)
    while rest > 0:
        candidates = [i for i in range(count - 1) if counts[i] < most]
        pool, remaining = sum([portions[i] for i in candidates]), rest
        for i in candidates:
            more = min(most - counts[i], max(1, remaining * portions[i] // pool), rest)
            counts[i] = counts[i] + more
            rest = rest - more
    return np.array([most] + counts)


def uneven(key, count, total, most, lean):
    if count == 2:
        one = jax.random.randint(key, (), max(1, total - most), min(most, total - 1) + 1)
        return jnp.stack([one, total - one])
    lengths = jnp.asarray(split_up(count, total, most, lean), jnp.int32)
    couples = (count - 1) // 2
    donor, receiver = lengths[1:1 + 2 * couples:2], lengths[2:2 + 2 * couples:2]
    margin = jnp.minimum(donor - 1, most - receiver)
    shifted = jax.random.randint(jax.random.fold_in(key, 1), (couples,), 0, 1 << 20) % (margin + 1)
    lengths = lengths.at[1:1 + 2 * couples:2].set(donor - shifted).at[2:2 + 2 * couples:2].set(receiver + shifted)
    return lengths[jax.random.permutation(jax.random.fold_in(key, 2), count)]


def bell_draw(stream_key, extent, scale, reach, pieces=(), held_as=jnp.bfloat16):
    factor_of = steps_of(stream_key, extent, pieces, -0.22, 0.18) if pieces else 1.0
    entries = jax.random.normal(stream_key, extent, jnp.float32) * scale * factor_of
    return jnp.minimum(jnp.maximum(entries, -reach), reach).astype(held_as)


def setup_inputs(seed: int = 0) -> dict:
    arg_keys = jax.random.split(jax.random.key(seed), 12)
    mixer_input = bell_draw(arg_keys[0], (SEQ, HEADS * HEAD_DIM), 1.0, 6.0, ((0, 32), (1, 4)))
    step_raw = draw_step_raw(jax.random.fold_in(arg_keys[11], 71), 0)
    step_bias = jnp.clip(-1.0 + 1.5 * jax.random.uniform(arg_keys[2], (HEADS,), jnp.float32) ** steps_of(arg_keys[2], (HEADS,), ((0, 4),), -0.2, 0.2), -1.0, 0.5)
    decay_log = draw_decay_log(jax.random.fold_in(arg_keys[11], 71), 0)
    skip_gain = jnp.clip(0.5 + 1.0 * jax.random.uniform(arg_keys[4], (HEADS,), jnp.float32) ** steps_of(arg_keys[4], (HEADS,), ((0, 4),), -0.2, 0.2), 0.5, 1.5)
    write_keys = bell_draw(arg_keys[5], (SEQ, GROUPS * DSTATE), (SEQ // 4) ** -0.5, 0.125, ((0, 32), (1, 4)))
    read_keys = bell_draw(arg_keys[6], (SEQ, GROUPS * DSTATE), DSTATE ** -0.5, 0.375, ((0, 32), (1, 4)))
    document_ids = jnp.searchsorted(jnp.cumsum(uneven(arg_keys[7], DOCS, SEQ, SEQ // 2, 0)), jnp.arange(SEQ), side="right").astype(jnp.int32)
    query_rows = draw_query_rows(jax.random.fold_in(arg_keys[11], 71), 0)
    key_rows = draw_key_rows(jax.random.fold_in(arg_keys[11], 71), 0)
    value_rows = bell_draw(arg_keys[10], (SEQ, KVHEADS * ATT_DIM), 1.0, 6.0, ((0, 128),))
    return dict(mixer_input=mixer_input, step_raw=step_raw, step_bias=step_bias, decay_log=decay_log, skip_gain=skip_gain, write_keys=write_keys, read_keys=read_keys, document_ids=document_ids, query_rows=query_rows, key_rows=key_rows, value_rows=value_rows)


highest = lax.Precision.HIGHEST
negative = -1e30


def mixer_block(step_bias, decay_log, skip_gain, carried, block):
    state, before = carried
    inputs, raw_steps, writes, readers, owners = block
    length = owners.shape[0]
    group_count = writes.shape[1]
    group_heads = inputs.shape[2]
    head_width = inputs.shape[3]
    stepsize = jax.nn.softplus(raw_steps + step_bias[None, :])
    logdec = -stepsize * jnp.exp(decay_log)[None, :]
    cumulative = jnp.cumsum(logdec, axis=0)
    places = jnp.arange(length)
    linked = (owners[:, None] == owners[None, :]) & (places[:, None] >= places[None, :])
    spread = cumulative.T[:, :, None] - cumulative.T[:, None, :]
    decays = jnp.where(linked[None], jnp.exp(jnp.minimum(spread, 0.0)), 0.0)
    scores = jnp.einsum("ign,jgn->gij", readers, writes, precision=highest)
    weights = decays.reshape(group_count, group_heads, length, length) * scores[:, None] * stepsize.T.reshape(group_count, group_heads, 1, length)
    inside = jnp.einsum("ghij,jghp->ighp", weights, inputs, precision=highest)
    entry_mask = (owners == before).astype(jnp.float32)
    factor = (jnp.exp(cumulative) * entry_mask[:, None]).reshape(length, group_count, group_heads, 1)
    carried_term = jnp.einsum("ign,ghpn->ighp", readers, state, precision=highest)
    output = inside + carried_term * factor + skip_gain.reshape(1, group_count, group_heads, 1) * inputs
    latest = owners[length - 1]
    trailing = jnp.where((owners == latest)[:, None], jnp.exp(cumulative[length - 1][None, :] - cumulative), 0.0) * stepsize
    written = jnp.einsum("jgh,jghp,jgn->ghpn", trailing.reshape(length, group_count, group_heads), inputs, writes, precision=highest)
    retain = (jnp.exp(cumulative[length - 1]) * (latest == before).astype(jnp.float32)).reshape(group_count, group_heads)
    state = retain[:, :, None, None] * state + written
    return (state, latest), output.reshape(length, group_count * group_heads * head_width).astype(jnp.bfloat16)


def attend_block(key_matrix, value_matrix, document_ids, scaling, element):
    queries, first_row, owners = element
    query_count = queries.shape[0]
    positions = first_row + jnp.arange(query_count, dtype=jnp.int32)
    scores = jnp.einsum("qgrd,kgd->grqk", queries.astype(jnp.float32), key_matrix) * scaling
    key_pos = jnp.arange(SEQ, dtype=jnp.int32)
    allowed = (key_pos[None, :] <= positions[:, None]) & (document_ids[None, :] == owners[:, None])
    masked = jnp.where(allowed, scores, negative)
    maxima = jnp.max(masked, axis=-1)
    weights = jnp.where(allowed, jnp.exp(masked - maxima[..., None]), 0.0)
    totals = jnp.sum(weights, axis=-1)
    rounded = lax.optimization_barrier(weights.astype(jnp.bfloat16)).astype(jnp.float32)
    summed = jnp.einsum("grqk,kgd->grqd", rounded, value_matrix)
    result = summed / totals[..., None]
    return result.transpose(2, 0, 1, 3).reshape(query_count, -1).astype(jnp.bfloat16)


def reference(mixer_input, step_raw, step_bias, decay_log, skip_gain, write_keys, read_keys, document_ids, query_rows, key_rows, value_rows):
    blocks = SEQ // TOK_DEV
    group_heads = HEADS // GROUPS
    inputs = mixer_input.astype(jnp.float32).reshape(blocks, TOK_DEV, GROUPS, group_heads, HEAD_DIM)
    raw_steps = step_raw.reshape(blocks, TOK_DEV, HEADS)
    writes = write_keys.astype(jnp.float32).reshape(blocks, TOK_DEV, GROUPS, DSTATE)
    readers = read_keys.astype(jnp.float32).reshape(blocks, TOK_DEV, GROUPS, DSTATE)
    owners = document_ids.reshape(blocks, TOK_DEV)
    initial = (jnp.zeros((GROUPS, group_heads, HEAD_DIM, DSTATE), jnp.float32), document_ids[0])
    folded, mixed = lax.scan(partial(mixer_block, step_bias, decay_log, skip_gain), initial, (inputs, raw_steps, writes, readers, owners))
    mixer_output = mixed.reshape(SEQ, HEADS * HEAD_DIM)
    query_block = 128 if SEQ % 128 == 0 else TOK_DEV
    query_blocks = SEQ // query_block
    repeats = QHEADS // KVHEADS
    queries = query_rows.reshape(query_blocks, query_block, KVHEADS, repeats, ATT_DIM)
    key_matrix = key_rows.astype(jnp.float32).reshape(SEQ, KVHEADS, ATT_DIM)
    value_matrix = value_rows.astype(jnp.float32).reshape(SEQ, KVHEADS, ATT_DIM)
    firsts = jnp.arange(query_blocks, dtype=jnp.int32) * query_block
    query_owners = document_ids.reshape(query_blocks, query_block)
    scaling = 1.0 / (ATT_DIM ** 0.5)
    attended = lax.map(partial(attend_block, key_matrix, value_matrix, document_ids, scaling), (queries, firsts, query_owners))
    attention_output = attended.reshape(SEQ, QHEADS * ATT_DIM)
    return mixer_output, attention_output
```

```python
import math

import jax
import jax.numpy as jnp
from jax import lax
from jax.experimental import pallas as pl
from jax.experimental.pallas import tpu as pltpu
from jax.sharding import PartitionSpec as P

TOKENS = 256
HEADS = 32
WIDTH = 64
DSTATE = 256
REPEATS = 8
DIM = 128
META = 16
ROWS = TOKENS + META
HALF = HEADS * WIDTH // 2
QUARTER = HALF // 4
CHUNK = 2 * TOKENS
BLOCKS = 32

f32 = jnp.float32
bf16 = jnp.bfloat16
highest = lax.Precision.HIGHEST
negative = -1e30


def context_place():
    position = lax.axis_index("context")
    return position // 8, (position // 2) % 4, position % 2


def run(kernel, name, outs, *args, scratch=(), mib=16, flops=0, transcendentals=0):
    moved = sum(math.prod(a.shape) * a.dtype.itemsize for a in args)
    moved += sum(math.prod(a.shape) * a.dtype.itemsize for a in outs)
    return pl.pallas_call(
        kernel,
        out_shape=outs,
        in_specs=[pl.BlockSpec(memory_space=pltpu.VMEM)] * len(args),
        out_specs=[pl.BlockSpec(memory_space=pltpu.VMEM)] * len(outs),
        scratch_shapes=list(scratch),
        compiler_params=pltpu.CompilerParams(vmem_limit_bytes=mib << 20),
        cost_estimate=pl.CostEstimate(
            flops=flops, bytes_accessed=moved, transcendentals=transcendentals
        ),
        name=name,
    )(*args)


def shape(rows, columns, dtype=bf16):
    return jax.ShapeDtypeStruct((rows, columns), dtype)


def iota(rows, columns, axis):
    return lax.broadcasted_iota(jnp.int32, (rows, columns), axis)


def split3(value):
    high = value.astype(bf16)
    rest = value - high.astype(f32)
    middle = rest.astype(bf16)
    low = (rest - middle.astype(f32)).astype(bf16)
    return high, middle, low


def spread_matrix(chunk):
    column = iota(HEADS, 256, 1) + 256 * chunk
    return (column // WIDTH == iota(HEADS, 256, 0)).astype(bf16)


def spread(value, matrix):
    high, middle, _ = split3(value)
    return jnp.dot(high, matrix, preferred_element_type=f32) + jnp.dot(
        middle, matrix, preferred_element_type=f32
    )


def document_column(docs_row):
    return jnp.broadcast_to(docs_row.astype(f32), (128, TOKENS)).T


def write_kernel(raw, bias, decay, docs, inputs, writes, mine, theirs, cum_out, offset_out):
    _, _, core = context_place()
    u = raw[...] + bias[...]
    step = jnp.maximum(u, 0.0) + jnp.log1p(jnp.exp(-jnp.abs(u)))
    logdec = -step * jnp.exp(decay[...])
    triangle = (iota(TOKENS, TOKENS, 0) >= iota(TOKENS, TOKENS, 1)).astype(f32)
    cum = jnp.dot(triangle, logdec, precision=highest, preferred_element_type=f32)
    cum_out[...] = cum
    offset = cum - jnp.log(step)
    padded = jnp.concatenate([offset, jnp.zeros((TOKENS, 128 - HEADS), f32)], axis=1)
    offset_out[...] = padded.T[:HEADS]
    total = cum[TOKENS - 1 :]
    column = document_column(docs[...])[:, :HEADS]
    last = column[TOKENS - 1 :]
    trail = jnp.where(column == last, jnp.exp(total - cum), 0.0) * step
    high, middle, low = [part.astype(f32) for part in split3(total)]
    row = iota(META, HEADS, 0)
    meta = jnp.where(
        row == 0,
        high,
        jnp.where(row == 1, middle, jnp.where(row == 2, low, jnp.where(row == 3, last, 0.0))),
    ).astype(bf16)
    turned = writes[...].T
    for chunk in range(8):
        matrix = spread_matrix(chunk)
        columns = slice(256 * chunk, 256 * (chunk + 1))
        scaled = (inputs[:, columns].astype(f32) * spread(trail, matrix)).astype(bf16)
        state = jnp.dot(turned, scaled, preferred_element_type=f32).astype(bf16)
        described = jnp.dot(meta, matrix, preferred_element_type=f32).astype(bf16)
        local = slice(256 * (chunk % 4), 256 * (chunk % 4 + 1))

        def store(ref):
            ref[:TOKENS, local] = state
            ref[TOKENS:, local] = described

        pl.when(core == chunk // 4)(lambda: store(mine))
        pl.when(core != chunk // 4)(lambda: store(theirs))


def inside_kernel(cum, offset, docs, inputs, writes, reads, gain, out):
    scores = lax.dot_general(
        reads[...], writes[...], (((1,), (1,)), ((), ())), preferred_element_type=f32
    )
    column = document_column(docs[...])
    column = jnp.concatenate([column, column], axis=1)
    linked = (column == docs[...].astype(f32)) & (
        iota(TOKENS, TOKENS, 0) >= iota(TOKENS, TOKENS, 1)
    )
    scores = jnp.where(linked, scores, 0.0)
    upper = scores[:128, :128]
    lower = scores[128:]
    left = iota(TOKENS, 128, 1) < WIDTH
    for pair in range(HEADS // 2):
        columns = slice(128 * pair, 128 * (pair + 1))
        u = inputs[:, columns]
        zero = jnp.zeros_like(u)
        top = bottom = None
        for side in range(2):
            head = 2 * pair + side
            part = jnp.where(left, u, zero) if side == 0 else jnp.where(left, zero, u)
            ci = cum[:, head : head + 1]
            cj = offset[head : head + 1, :]
            first = (jnp.exp(ci[:128] - cj[:, :128]) * upper).astype(bf16)
            second = (jnp.exp(ci[128:] - cj) * lower).astype(bf16)
            first = jnp.dot(first, part[:128], preferred_element_type=f32)
            second = jnp.dot(second, part, preferred_element_type=f32)
            top = first if top is None else top + first
            bottom = second if bottom is None else bottom + second
        gains = jnp.where(
            left[:1], gain[:, 2 * pair : 2 * pair + 1], gain[:, 2 * pair + 1 : 2 * pair + 2]
        )
        wide = u.astype(f32) * gains
        out[:128, columns] = top + wide[:128]
        out[128:, columns] = bottom + wide[128:]


def described(ref_rows):
    rows = ref_rows.astype(f32)
    return rows[0:1] + rows[1:2] + rows[2:3], rows[3:4]


def meta_rows(total, last):
    high, middle, low = [part.astype(f32) for part in split3(total)]
    row = iota(META, total.shape[1], 0)
    return jnp.where(
        row == 0,
        high,
        jnp.where(row == 1, middle, jnp.where(row == 2, low, jnp.where(row == 3, last, 0.0))),
    ).astype(bf16)


def joined(earlier, later):
    total = earlier[1] + later[1]
    keep = jnp.where(later[2] == earlier[2], jnp.exp(later[1]), 0.0)
    return keep * earlier[0] + later[0], total, later[2]


def unpacked(payload):
    total, last = described(payload[TOKENS:])
    return payload[:TOKENS].astype(f32), total, last


def chip_kernel(mine, other, *outs):
    _, z, core = context_place()
    for step in range(4):
        columns = pl.ds(pl.multiple_of(((z + step) % 4) * QUARTER, QUARTER), QUARTER)
        own, near = mine[:, columns], other[:, columns]
        first = unpacked(jnp.where(core == 0, own, near))
        second = unpacked(jnp.where(core == 0, near, own))
        state, total, last = joined(first, second)
        outs[step][:TOKENS] = state.astype(bf16)
        outs[step][TOKENS:] = meta_rows(total, last)


def picked(slots, index):
    value = slots[0]
    for number in range(1, len(slots)):
        value = jnp.where(index == number, slots[number], value)
    return value


def row_kernel(a0, a1, a2, a3, out):
    _, z, _ = context_place()
    slots = [ref[...] for ref in (a0, a1, a2, a3)]
    whole = unpacked(picked(slots, z))
    for chip in range(1, 4):
        whole = joined(whole, unpacked(picked(slots, (z - chip) % 4)))
    out[:TOKENS] = whole[0].astype(bf16)
    out[TOKENS:] = meta_rows(whole[1], whole[2])


def entering_kernel(a0, a1, a2, a3, near, far, *outs):
    _, z, _ = context_place()
    slots = [ref[...] for ref in (a0, a1, a2, a3)]
    current = joined(unpacked(far[...]), unpacked(near[...]))
    entering = []
    for chip in range(4):
        entering.append((current[0].astype(bf16), meta_rows(current[1], current[2])))
        if chip < 3:
            current = joined(current, unpacked(picked(slots, (z - chip) % 4)))
    for step in range(4):
        outs[step][:TOKENS] = picked([e[0] for e in entering], (z + step) % 4)
        outs[step][TOKENS:] = picked([e[1] for e in entering], (z + step) % 4)


def core_kernel(b0, b1, b2, b3, mine, other, keep, send):
    _, z, core = context_place()
    for step, ref in enumerate((b0, b1, b2, b3)):
        columns = pl.ds(pl.multiple_of(((z - step) % 4) * QUARTER, QUARTER), QUARTER)
        first = ref[...]
        written = unpacked(jnp.where(core == 0, mine[:, columns], other[:, columns]))
        state, total, last = joined(unpacked(first), written)
        second = jnp.concatenate([state.astype(bf16), meta_rows(total, last)], axis=0)
        keep[:, columns] = jnp.where(core == 0, first, second)
        send[:, columns] = jnp.where(core == 0, second, first)


def carried_kernel(inside, cum, docs, reads, keep, other, out):
    _, _, core = context_place()
    before = keep[TOKENS:, :HEADS][3:4].astype(f32)
    column = document_column(docs[...])[:, :HEADS]
    factor = jnp.where(column == before, jnp.exp(cum[...]), 0.0)
    for chunk in range(8):
        columns = slice(256 * chunk, 256 * (chunk + 1))
        local = slice(256 * (chunk % 4), 256 * (chunk % 4 + 1))
        state = jnp.where(core == chunk // 4, keep[:TOKENS, local], other[:TOKENS, local])
        carried = jnp.dot(reads[...], state, preferred_element_type=f32)
        scale = spread(factor, spread_matrix(chunk))
        out[:, columns] = (inside[:, columns] + carried * scale).astype(bf16)


def cut_kernel(keys, values, *outs):
    x = lax.axis_index("tensor")
    for step in range(4):
        columns = pl.ds(pl.multiple_of(((x + step) % 4) * DIM, DIM), DIM)
        outs[step][:, :DIM] = keys[:, columns]
        outs[step][:, DIM:] = values[:, columns]


def assemble_kernel(p0, p1, p2, p3, docs, out):
    x = lax.axis_index("tensor")
    for step, ref in enumerate((p0, p1, p2, p3)):
        out[pl.ds(pl.multiple_of(((x - step) % 4) * 64, 64), 64), :] = ref[...]
    first = jnp.sum(jnp.where(docs[...] < 1, 1.0, 0.0), axis=1, keepdims=True)
    second = jnp.sum(jnp.where(docs[...] < 2, 1.0, 0.0), axis=1, keepdims=True)
    lane = iota(META, 2 * DIM, 1)
    out[TOKENS:] = jnp.where(lane == 0, first, jnp.where(lane == 1, second, 0.0)).astype(bf16)


def attention_kernel(queries, docs, gathered, out, turned, peaks, sums):
    position = lax.axis_index("context")
    base = position * TOKENS
    ids = docs[...]
    counts = jnp.zeros((META, 128), f32)
    for block in range(BLOCKS):
        counts = counts + gathered[block * ROWS + TOKENS : (block + 1) * ROWS, :128].astype(f32)
    row, lane = iota(META, 128, 0), iota(META, 128, 1)
    below_one = jnp.sum(jnp.where((row == 0) & (lane == 0), counts, 0.0)).astype(jnp.int32)
    below_two = jnp.sum(jnp.where((row == 0) & (lane == 1), counts, 0.0)).astype(jnp.int32)
    opening = jnp.min(ids)
    start = jnp.where(opening == 0, 0, jnp.where(opening == 1, below_one, below_two))
    own_one = jnp.sum(jnp.where(ids < 1, 1.0, 0.0)).astype(jnp.int32)
    own_two = jnp.sum(jnp.where(ids < 2, 1.0, 0.0)).astype(jnp.int32)
    lowest = jnp.where(ids == opening, start, base + jnp.where(ids == 1, own_one, own_two))
    highest_start = jnp.max(lowest)
    token = base + iota(1, TOKENS, 1)

    factor = math.log2(math.e) / math.sqrt(DIM)
    for head in range(REPEATS):
        scaled = (queries[:, head * DIM : (head + 1) * DIM].astype(f32) * factor).T
        high, middle, _ = split3(scaled)
        turned[head, :DIM] = high
        turned[head, DIM:] = middle
    peaks[...] = jnp.full_like(peaks, negative)
    sums[...] = jnp.zeros_like(sums)

    def fold(chunk, masked):
        begin = pl.multiple_of(chunk * 2 * ROWS, 2 * ROWS)
        one = gathered[pl.ds(begin, TOKENS), :]
        two = gathered[pl.ds(pl.multiple_of(begin + ROWS, ROWS), TOKENS), :]
        keys = jnp.concatenate([one[:, :DIM], two[:, :DIM]], axis=0)
        keys = jnp.concatenate([keys, keys], axis=1)
        values = jnp.concatenate([one[:, DIM:], two[:, DIM:]], axis=0)
        values = jnp.concatenate([values.T, jnp.ones((META, CHUNK), bf16)], axis=0)
        if masked:
            place = chunk * CHUNK + iota(CHUNK, TOKENS, 0)
            allowed = (place <= token) & (place >= lowest)
            bias = jnp.where(allowed, 0.0, negative)
        for head in range(REPEATS):
            scores = jnp.dot(keys, turned[head], preferred_element_type=f32)
            if masked:
                scores = scores + bias
            old = peaks[head : head + 1]
            new = jnp.maximum(old, jnp.max(scores, axis=0, keepdims=True))
            weights = jnp.exp2(scores - new).astype(bf16)
            peaks[head : head + 1] = new
            sums[head] = sums[head] * jnp.exp2(old - new) + jnp.dot(
                values, weights, preferred_element_type=f32
            )

    first = start // CHUNK
    last = position // 2
    clear = jnp.minimum((highest_start + CHUNK - 1) // CHUNK, last)
    edges = clear - first

    @pl.loop(0, edges + 1)
    def _(number):
        fold(jnp.where(number < edges, first + number, last), True)

    @pl.loop(clear, last)
    def _(chunk):
        fold(chunk, False)

    for head in range(REPEATS):
        result = sums[head, :DIM] * (1.0 / sums[head, DIM : DIM + 1])
        out[:, head * DIM : (head + 1) * DIM] = result.T.astype(bf16)


def around_z(steps):
    return [
        (y * 8 + z * 2 + k, y * 8 + ((z + steps) % 4) * 2 + k)
        for y in range(4)
        for z in range(4)
        for k in range(2)
    ]


def along_y(steps):
    return [(c, c + 8 * steps) for c in range(BLOCKS - 8 * steps)]


def body(
    mixer_input,
    step_raw,
    step_bias,
    decay_log,
    skip_gain,
    write_keys,
    read_keys,
    document_ids,
    query_rows,
    key_rows,
    value_rows,
):
    docs = document_ids.reshape(1, TOKENS)
    across = [(c, c ^ 1) for c in range(BLOCKS)]

    cuts = run(cut_kernel, "cut_keys", [shape(64, 2 * DIM)] * 4, key_rows, value_rows)
    parts = [cuts[0]] + [
        lax.ppermute(cuts[step], "tensor", [(x, (x + step) % 4) for x in range(4)])
        for step in (1, 2, 3)
    ]

    mine, theirs, cum, offset = run(
        write_kernel,
        "mixer_write",
        [shape(ROWS, HALF), shape(ROWS, HALF), shape(TOKENS, HEADS, f32), shape(HEADS, TOKENS, f32)],
        step_raw,
        step_bias.reshape(1, HEADS),
        decay_log.reshape(1, HEADS),
        docs,
        mixer_input,
        write_keys,
        mib=24,
        flops=2 * 256 * 256 * 2048,
    )
    other = lax.ppermute(theirs, "context", across)

    (block,) = run(assemble_kernel, "assemble_keys", [shape(ROWS, 2 * DIM)], *parts, docs)
    gathered = lax.all_gather(block, "context", axis=0, tiled=True)

    quarter = [shape(ROWS, QUARTER)]
    chips = run(chip_kernel, "chip_state", quarter * 4, mine, other)
    slots = [chips[0]] + [lax.ppermute(chips[s], "context", around_z(s)) for s in (1, 2, 3)]

    (inside,) = run(
        inside_kernel,
        "mixer_inside",
        [shape(TOKENS, HEADS * WIDTH, f32)],
        cum,
        offset,
        docs,
        mixer_input,
        write_keys,
        read_keys,
        skip_gain.reshape(1, HEADS),
        mib=24,
        flops=2 * 256 * 256 * 128 * 32,
    )

    (row,) = run(row_kernel, "row_state", quarter, *slots)
    near = lax.ppermute(row, "context", along_y(1))
    far = lax.ppermute(row, "context", along_y(2))
    entering = run(entering_kernel, "entering_state", quarter * 4, *slots, near, far)
    back = [entering[0]] + [lax.ppermute(entering[s], "context", around_z(s)) for s in (1, 2, 3)]
    keep, send = run(core_kernel, "core_state", [shape(ROWS, HALF)] * 2, *back, mine, other)
    arrived = lax.ppermute(send, "context", across)
    (mixed,) = run(
        carried_kernel,
        "mixer_carried",
        [shape(TOKENS, HEADS * WIDTH)],
        inside,
        cum,
        docs,
        read_keys,
        keep,
        arrived,
        mib=24,
        flops=2 * 256 * 256 * 2048,
    )

    (attended,) = run(
        attention_kernel,
        "attention",
        [shape(TOKENS, REPEATS * DIM)],
        query_rows,
        docs,
        gathered,
        scratch=[
            pltpu.VMEM((REPEATS, 2 * DIM, TOKENS), bf16),
            pltpu.VMEM((REPEATS, TOKENS), f32),
            pltpu.VMEM((REPEATS, DIM + META, TOKENS), f32),
        ],
        mib=32,
        flops=4 * 2048 * 4096 * 128,
        transcendentals=2048 * 4096,
    )
    return mixed, attended


def solution(mesh):
    placed = (
        P("context", "tensor"),
        P("context", "tensor"),
        P("tensor"),
        P("tensor"),
        P("tensor"),
        P("context", "tensor"),
        P("context", "tensor"),
        P("context"),
        P("context", "tensor"),
        P(("context", "tensor"), None),
        P(("context", "tensor"), None),
    )
    return jax.shard_map(
        body,
        mesh=mesh,
        in_specs=placed,
        out_specs=(P("context", "tensor"), P("context", "tensor")),
        check_vma=False,
    )
```

```python
import math

import jax
import jax.numpy as jnp
from jax import lax
from jax.experimental import pallas as pl
from jax.experimental.pallas import tpu as pltpu
from jax.sharding import PartitionSpec as P

TOKENS = 256
HEADS = 32
WIDTH = 64
DSTATE = 256
REPEATS = 8
DIM = 128
META = 16
ROWS = TOKENS + META
HALF = HEADS * WIDTH // 2
QUARTER = HALF // 4
CHUNK = 2 * TOKENS
BLOCKS = 32
LEAD = 3

f32 = jnp.float32
bf16 = jnp.bfloat16
highest = lax.Precision.HIGHEST
negative = -1e30


def context_place():
    position = lax.axis_index("context")
    return position // 8, (position // 2) % 4, position % 2


def run(kernel, name, outs, *args, far=(), scratch=(), mib=16, flops=0, transcendentals=0):
    moved = sum(math.prod(a.shape) * a.dtype.itemsize for a in args)
    moved += sum(math.prod(a.shape) * a.dtype.itemsize for a in outs)
    spaces = [pltpu.HBM if number in far else pltpu.VMEM for number in range(len(args))]
    return pl.pallas_call(
        kernel,
        out_shape=outs,
        in_specs=[pl.BlockSpec(memory_space=space) for space in spaces],
        out_specs=[pl.BlockSpec(memory_space=pltpu.VMEM)] * len(outs),
        scratch_shapes=list(scratch),
        compiler_params=pltpu.CompilerParams(vmem_limit_bytes=mib << 20),
        cost_estimate=pl.CostEstimate(
            flops=flops, bytes_accessed=moved, transcendentals=transcendentals
        ),
        name=name,
    )(*args)


def shape(rows, columns, dtype=bf16):
    return jax.ShapeDtypeStruct((rows, columns), dtype)


def iota(rows, columns, axis):
    return lax.broadcasted_iota(jnp.int32, (rows, columns), axis)


def split3(value):
    high = value.astype(bf16)
    rest = value - high.astype(f32)
    middle = rest.astype(bf16)
    low = (rest - middle.astype(f32)).astype(bf16)
    return high, middle, low


def spread_matrix(chunk):
    column = iota(HEADS, 256, 1) + 256 * chunk
    return (column // WIDTH == iota(HEADS, 256, 0)).astype(bf16)


def spread(value, matrix):
    high, middle, _ = split3(value)
    return jnp.dot(high, matrix, preferred_element_type=f32) + jnp.dot(
        middle, matrix, preferred_element_type=f32
    )


def document_column(docs_row):
    return jnp.broadcast_to(docs_row.astype(f32), (128, TOKENS)).T


def fetch(sources, targets, semaphores):
    copies = [
        pltpu.make_async_copy(source, target, semaphores.at[number])
        for number, (source, target) in enumerate(zip(sources, targets))
    ]
    for copy in copies:
        copy.start()
    return copies


def write_kernel(*refs):
    far, (mine, theirs, cum_out, offset_out), held, semaphores = refs[:6], refs[6:10], refs[10:16], refs[16]
    copies = fetch(far, held, semaphores)
    raw, bias, decay, docs, inputs, writes = held
    _, _, core = context_place()
    for copy in copies[:4]:
        copy.wait()
    u = raw[...] + bias[...]
    step = jnp.maximum(u, 0.0) + jnp.log1p(jnp.exp(-jnp.abs(u)))
    logdec = -step * jnp.exp(decay[...])
    triangle = (iota(TOKENS, TOKENS, 0) >= iota(TOKENS, TOKENS, 1)).astype(f32)
    cum = jnp.dot(triangle, logdec, precision=highest, preferred_element_type=f32)
    cum_out[...] = cum
    offset = cum - jnp.log(step)
    padded = jnp.concatenate([offset, jnp.zeros((TOKENS, 128 - HEADS), f32)], axis=1)
    offset_out[...] = padded.T[:HEADS]
    total = cum[TOKENS - 1 :]
    column = document_column(docs[...])[:, :HEADS]
    last = column[TOKENS - 1 :]
    trail = jnp.where(column == last, jnp.exp(total - cum), 0.0) * step
    high, middle, low = [part.astype(f32) for part in split3(total)]
    row = iota(META, HEADS, 0)
    meta = jnp.where(
        row == 0,
        high,
        jnp.where(row == 1, middle, jnp.where(row == 2, low, jnp.where(row == 3, last, 0.0))),
    ).astype(bf16)
    copies[5].wait()
    turned = writes[...].T
    copies[4].wait()
    for chunk in range(8):
        matrix = spread_matrix(chunk)
        columns = slice(256 * chunk, 256 * (chunk + 1))
        scaled = (inputs[:, columns].astype(f32) * spread(trail, matrix)).astype(bf16)
        state = jnp.dot(turned, scaled, preferred_element_type=f32).astype(bf16)
        described = jnp.dot(meta, matrix, preferred_element_type=f32).astype(bf16)
        local = slice(256 * (chunk % 4), 256 * (chunk % 4 + 1))

        def store(ref):
            ref[:TOKENS, local] = state
            ref[TOKENS:, local] = described

        pl.when(core == chunk // 4)(lambda: store(mine))
        pl.when(core != chunk // 4)(lambda: store(theirs))


def inside_kernel(cum, offset, docs, inputs, writes, reads, gain, out):
    scores = lax.dot_general(
        reads[...], writes[...], (((1,), (1,)), ((), ())), preferred_element_type=f32
    )
    column = document_column(docs[...])
    column = jnp.concatenate([column, column], axis=1)
    linked = (column == docs[...].astype(f32)) & (
        iota(TOKENS, TOKENS, 0) >= iota(TOKENS, TOKENS, 1)
    )
    scores = jnp.where(linked, scores, 0.0)
    upper = scores[:128, :128]
    lower = scores[128:]
    left = iota(TOKENS, 128, 1) < WIDTH
    for pair in range(HEADS // 2):
        columns = slice(128 * pair, 128 * (pair + 1))
        u = inputs[:, columns]
        zero = jnp.zeros_like(u)
        top = bottom = None
        for side in range(2):
            head = 2 * pair + side
            part = jnp.where(left, u, zero) if side == 0 else jnp.where(left, zero, u)
            ci = cum[:, head : head + 1]
            cj = offset[head : head + 1, :]
            first = (jnp.exp(ci[:128] - cj[:, :128]) * upper).astype(bf16)
            second = (jnp.exp(ci[128:] - cj) * lower).astype(bf16)
            first = jnp.dot(first, part[:128], preferred_element_type=f32)
            second = jnp.dot(second, part, preferred_element_type=f32)
            top = first if top is None else top + first
            bottom = second if bottom is None else bottom + second
        gains = jnp.where(
            left[:1], gain[:, 2 * pair : 2 * pair + 1], gain[:, 2 * pair + 1 : 2 * pair + 2]
        )
        wide = u.astype(f32) * gains
        out[:128, columns] = top + wide[:128]
        out[128:, columns] = bottom + wide[128:]


def described(ref_rows):
    rows = ref_rows.astype(f32)
    return rows[0:1] + rows[1:2] + rows[2:3], rows[3:4]


def meta_rows(total, last):
    high, middle, low = [part.astype(f32) for part in split3(total)]
    row = iota(META, total.shape[1], 0)
    return jnp.where(
        row == 0,
        high,
        jnp.where(row == 1, middle, jnp.where(row == 2, low, jnp.where(row == 3, last, 0.0))),
    ).astype(bf16)


def joined(earlier, later):
    total = earlier[1] + later[1]
    keep = jnp.where(later[2] == earlier[2], jnp.exp(later[1]), 0.0)
    return keep * earlier[0] + later[0], total, later[2]


def unpacked(payload):
    total, last = described(payload[TOKENS:])
    return payload[:TOKENS].astype(f32), total, last


def chip_kernel(mine, other, *outs):
    _, z, core = context_place()
    for step in range(4):
        columns = pl.ds(pl.multiple_of(((z + step) % 4) * QUARTER, QUARTER), QUARTER)
        own, near = mine[:, columns], other[:, columns]
        first = unpacked(jnp.where(core == 0, own, near))
        second = unpacked(jnp.where(core == 0, near, own))
        state, total, last = joined(first, second)
        outs[step][:TOKENS] = state.astype(bf16)
        outs[step][TOKENS:] = meta_rows(total, last)


def picked(slots, index):
    value = slots[0]
    for number in range(1, len(slots)):
        value = jnp.where(index == number, slots[number], value)
    return value


def row_kernel(a0, a1, a2, a3, out):
    _, z, _ = context_place()
    slots = [ref[...] for ref in (a0, a1, a2, a3)]
    whole = unpacked(picked(slots, z))
    for chip in range(1, 4):
        whole = joined(whole, unpacked(picked(slots, (z - chip) % 4)))
    out[:TOKENS] = whole[0].astype(bf16)
    out[TOKENS:] = meta_rows(whole[1], whole[2])


def entering_kernel(a0, a1, a2, a3, near, far, *outs):
    _, z, _ = context_place()
    slots = [ref[...] for ref in (a0, a1, a2, a3)]
    current = joined(unpacked(far[...]), unpacked(near[...]))
    entering = []
    for chip in range(4):
        entering.append((current[0].astype(bf16), meta_rows(current[1], current[2])))
        if chip < 3:
            current = joined(current, unpacked(picked(slots, (z - chip) % 4)))
    for step in range(4):
        outs[step][:TOKENS] = picked([e[0] for e in entering], (z + step) % 4)
        outs[step][TOKENS:] = picked([e[1] for e in entering], (z + step) % 4)


def core_kernel(b0, b1, b2, b3, mine, other, keep, send):
    _, z, core = context_place()
    for step, ref in enumerate((b0, b1, b2, b3)):
        columns = pl.ds(pl.multiple_of(((z - step) % 4) * QUARTER, QUARTER), QUARTER)
        first = ref[...]
        written = unpacked(jnp.where(core == 0, mine[:, columns], other[:, columns]))
        state, total, last = joined(unpacked(first), written)
        second = jnp.concatenate([state.astype(bf16), meta_rows(total, last)], axis=0)
        keep[:, columns] = jnp.where(core == 0, first, second)
        send[:, columns] = jnp.where(core == 0, second, first)


def carried_kernel(inside, cum, docs, reads, keep, other, out):
    _, _, core = context_place()
    before = keep[TOKENS:, :HEADS][3:4].astype(f32)
    column = document_column(docs[...])[:, :HEADS]
    factor = jnp.where(column == before, jnp.exp(cum[...]), 0.0)
    for chunk in range(8):
        columns = slice(256 * chunk, 256 * (chunk + 1))
        local = slice(256 * (chunk % 4), 256 * (chunk % 4 + 1))
        state = jnp.where(core == chunk // 4, keep[:TOKENS, local], other[:TOKENS, local])
        carried = jnp.dot(reads[...], state, preferred_element_type=f32)
        scale = spread(factor, spread_matrix(chunk))
        out[:, columns] = (inside[:, columns] + carried * scale).astype(bf16)


def cut_kernel(keys, values, *refs):
    outs, semaphores = refs[:4], refs[4]
    x = lax.axis_index("tensor")
    sources, targets = [], []
    for step in range(4):
        columns = pl.ds(pl.multiple_of(((x + step) % 4) * DIM, DIM), DIM)
        sources += [keys.at[:, columns], values.at[:, columns]]
        targets += [outs[step].at[:, :DIM], outs[step].at[:, DIM:]]
    for copy in fetch(sources, targets, semaphores):
        copy.wait()


def assemble_kernel(p0, p1, p2, p3, docs, out):
    x = lax.axis_index("tensor")
    for step, ref in enumerate((p0, p1, p2, p3)):
        out[pl.ds(pl.multiple_of(((x - step) % 4) * 64, 64), 64), :] = ref[...]
    first = jnp.sum(jnp.where(docs[...] >= 1, 1.0, 0.0), axis=1, keepdims=True)
    second = jnp.sum(jnp.where(docs[...] >= 2, 1.0, 0.0), axis=1, keepdims=True)
    lane = iota(META, 2 * DIM, 1)
    counts = jnp.where(lane == 1, first, jnp.where(lane == 2, second, 0.0))
    out[TOKENS:] = jnp.where(lane == 0, float(TOKENS), counts).astype(bf16)


def chunk_kernel(mine, other, out):
    _, _, core = context_place()
    out[:ROWS] = jnp.where(core == 0, mine[...], other[...])
    out[ROWS:] = jnp.where(core == 0, other[...], mine[...])


def far_kernel(chunk, above, *outs):
    _, z, core = context_place()
    for step in range(1, 4):
        own = (core == 1) & ((z + step) % 4 > z)
        outs[step - 1][...] = jnp.where(own, chunk[...], above[...])


def bundle_kernel(a0, a1, a2, a3, out):
    for step, ref in enumerate((a0, a1, a2, a3)):
        out[2 * ROWS * step : 2 * ROWS * (step + 1)] = ref[...]


def attention_kernel(queries, docs, chunk_ref, bundle, arrived, out, turned, peaks, sums):
    y, z, core = context_place()
    base = lax.axis_index("context") * TOKENS
    own = y * 4 + z
    ids = docs[...]
    opening = jnp.min(ids)
    counts = jnp.where(core == 1, chunk_ref[TOKENS:ROWS, :128].astype(f32), 0.0)
    for block in range(8):
        rows = slice(block * ROWS + TOKENS, (block + 1) * ROWS)
        counts = counts + bundle[rows, :128].astype(f32) + arrived[rows, :128].astype(f32)
    here = (iota(META, 128, 0) == 0) & (iota(META, 128, 1) == opening)
    start = base - jnp.sum(jnp.where(here, counts, 0.0)).astype(jnp.int32)
    below_two = jnp.sum(jnp.where(ids < 2, 1.0, 0.0)).astype(jnp.int32)
    below_one = jnp.sum(jnp.where(ids < 1, 1.0, 0.0)).astype(jnp.int32)
    lowest = jnp.where(ids == opening, start, base + jnp.where(ids == 1, below_one, below_two))
    highest_start = jnp.max(lowest)
    token = base + iota(1, TOKENS, 1)

    factor = math.log2(math.e) / math.sqrt(DIM)
    for head in range(REPEATS):
        scaled = (queries[:, head * DIM : (head + 1) * DIM].astype(f32) * factor).T
        high, middle, _ = split3(scaled)
        turned[head, :DIM] = high
        turned[head, DIM:] = middle
    peaks[...] = jnp.full_like(peaks, negative)
    sums[...] = jnp.zeros_like(sums)

    def rows_of(chunk, masked):
        near = chunk // 4 == y - 1
        slot = ((z - chunk) % 4) * 2 * ROWS
        found = []
        for block in range(2):
            place = pl.ds(pl.multiple_of(slot + block * ROWS, ROWS), TOKENS)
            rows = jnp.where(near == (core == 0), bundle[place, :], arrived[place, :])
            if masked:
                rows = jnp.where(chunk == own, chunk_ref[block * ROWS : block * ROWS + TOKENS], rows)
            found.append(rows)
        return found

    def fold(chunk, masked):
        one, two = rows_of(chunk, masked)
        keys = jnp.concatenate([one[:, :DIM], two[:, :DIM]], axis=0)
        keys = jnp.concatenate([keys, keys], axis=1)
        values = jnp.concatenate([one[:, DIM:], two[:, DIM:]], axis=0)
        values = jnp.concatenate([values.T, jnp.ones((META, CHUNK), bf16)], axis=0)
        if masked:
            place = chunk * CHUNK + iota(CHUNK, TOKENS, 0)
            allowed = (place <= token) & (place >= lowest)
            bias = jnp.where(allowed, 0.0, negative)

        def score(head):
            scores = jnp.dot(keys, turned[head], preferred_element_type=f32)
            return scores + bias if masked else scores

        def add(head, weights, shrink):
            sums[head] = sums[head] * shrink + jnp.dot(
                values, weights, preferred_element_type=f32
            )

        ahead = [score(head) for head in range(LEAD)]
        pending = None
        for head in range(REPEATS):
            if head + LEAD < REPEATS:
                ahead.append(score(head + LEAD))
            scores = ahead[head]
            old = peaks[head : head + 1]
            new = jnp.maximum(old, jnp.max(scores, axis=0, keepdims=True))
            weights = jnp.exp2(scores - new).astype(bf16)
            peaks[head : head + 1] = new
            if pending is not None:
                add(*pending)
            pending = (head, weights, jnp.exp2(old - new))
        add(*pending)

    first = start // CHUNK
    clear = jnp.minimum((highest_start + CHUNK - 1) // CHUNK, own)
    edges = clear - first

    @pl.loop(0, edges + 1)
    def _(number):
        fold(jnp.where(number < edges, first + number, own), True)

    @pl.loop(clear, own)
    def _(chunk):
        fold(chunk, False)

    for head in range(REPEATS):
        result = sums[head, :DIM] * (1.0 / sums[head, DIM : DIM + 1])
        out[:, head * DIM : (head + 1) * DIM] = result.T.astype(bf16)


def around_z(steps):
    return [
        (y * 8 + z * 2 + k, y * 8 + ((z + steps) % 4) * 2 + k)
        for y in range(4)
        for z in range(4)
        for k in range(2)
    ]


def along_y(steps):
    return [(c, c + 8 * steps) for c in range(BLOCKS - 8 * steps)]


def body(
    mixer_input,
    step_raw,
    step_bias,
    decay_log,
    skip_gain,
    write_keys,
    read_keys,
    document_ids,
    query_rows,
    key_rows,
    value_rows,
):
    docs = document_ids.reshape(1, TOKENS)
    across = [(c, c ^ 1) for c in range(BLOCKS)]
    below = [(c, c + 8 * (1 + c % 2)) for c in range(BLOCKS) if c + 8 * (1 + c % 2) < BLOCKS]

    cuts = run(
        cut_kernel,
        "cut_keys",
        [shape(64, 2 * DIM)] * 4,
        key_rows,
        value_rows,
        far=(0, 1),
        scratch=[pltpu.SemaphoreType.DMA((8,))],
    )
    parts = [cuts[0]] + [
        lax.ppermute(cuts[step], "tensor", [(x, (x + step) % 4) for x in range(4)])
        for step in (1, 2, 3)
    ]

    mine, theirs, cum, offset = run(
        write_kernel,
        "mixer_write",
        [shape(ROWS, HALF), shape(ROWS, HALF), shape(TOKENS, HEADS, f32), shape(HEADS, TOKENS, f32)],
        step_raw,
        step_bias.reshape(1, HEADS),
        decay_log.reshape(1, HEADS),
        docs,
        mixer_input,
        write_keys,
        far=range(6),
        scratch=[
            pltpu.VMEM((TOKENS, HEADS), f32),
            pltpu.VMEM((1, HEADS), f32),
            pltpu.VMEM((1, HEADS), f32),
            pltpu.VMEM((1, TOKENS), jnp.int32),
            pltpu.VMEM((TOKENS, HEADS * WIDTH), bf16),
            pltpu.VMEM((TOKENS, DSTATE), bf16),
            pltpu.SemaphoreType.DMA((6,)),
        ],
        mib=24,
        flops=2 * 256 * 256 * 2048,
    )
    (block,) = run(assemble_kernel, "assemble_keys", [shape(ROWS, 2 * DIM)], *parts, docs)
    other_block = lax.ppermute(block, "context", across)
    other = lax.ppermute(theirs, "context", across)

    (chunk,) = run(chunk_kernel, "chunk_keys", [shape(2 * ROWS, 2 * DIM)], block, other_block)
    above = lax.ppermute(chunk, "context", below)

    quarter = [shape(ROWS, QUARTER)]
    chips = run(chip_kernel, "chip_state", quarter * 4, mine, other)
    slots = [chips[0]] + [lax.ppermute(chips[s], "context", around_z(s)) for s in (1, 2, 3)]

    (inside,) = run(
        inside_kernel,
        "mixer_inside",
        [shape(TOKENS, HEADS * WIDTH, f32)],
        cum,
        offset,
        docs,
        mixer_input,
        write_keys,
        read_keys,
        skip_gain.reshape(1, HEADS),
        mib=24,
        flops=2 * 256 * 256 * 128 * 32,
    )

    far_cuts = run(far_kernel, "far_keys", [shape(2 * ROWS, 2 * DIM)] * 3, chunk, above)
    far = [lax.ppermute(far_cuts[s - 1], "context", around_z(s)) for s in (1, 2, 3)]

    slots, inside = lax.optimization_barrier((slots, inside))
    (row,) = run(row_kernel, "row_state", quarter, *slots)
    near_row = lax.ppermute(row, "context", along_y(1))
    far_row = lax.ppermute(row, "context", along_y(2))

    (bundle,) = run(bundle_kernel, "bundle_keys", [shape(8 * ROWS, 2 * DIM)], above, *far)
    arrived = lax.ppermute(bundle, "context", across)

    entering = run(entering_kernel, "entering_state", quarter * 4, *slots, near_row, far_row)
    back = [entering[0]] + [lax.ppermute(entering[s], "context", around_z(s)) for s in (1, 2, 3)]

    (attended,) = run(
        attention_kernel,
        "attention",
        [shape(TOKENS, REPEATS * DIM)],
        query_rows,
        docs,
        chunk,
        bundle,
        arrived,
        scratch=[
            pltpu.VMEM((REPEATS, 2 * DIM, TOKENS), bf16),
            pltpu.VMEM((REPEATS, TOKENS), f32),
            pltpu.VMEM((REPEATS, DIM + META, TOKENS), f32),
        ],
        mib=32,
        flops=4 * 2048 * 4096 * 128,
        transcendentals=2048 * 4096,
    )

    keep, send = run(core_kernel, "core_state", [shape(ROWS, HALF)] * 2, *back, mine, other)
    state_arrived = lax.ppermute(send, "context", across)
    (mixed,) = run(
        carried_kernel,
        "mixer_carried",
        [shape(TOKENS, HEADS * WIDTH)],
        inside,
        cum,
        docs,
        read_keys,
        keep,
        state_arrived,
        mib=24,
        flops=2 * 256 * 256 * 2048,
    )
    return mixed, attended


def solution(mesh):
    placed = (
        P("context", "tensor"),
        P("context", "tensor"),
        P("tensor"),
        P("tensor"),
        P("tensor"),
        P("context", "tensor"),
        P("context", "tensor"),
        P("context"),
        P("context", "tensor"),
        P(("context", "tensor"), None),
        P(("context", "tensor"), None),
    )
    return jax.shard_map(
        body,
        mesh=mesh,
        in_specs=placed,
        out_specs=(P("context", "tensor"), P("context", "tensor")),
        check_vma=False,
    )
```

```python
import math

import jax
import jax.numpy as jnp
from jax import lax
from jax.experimental import pallas as pl
from jax.experimental.pallas import tpu as pltpu
from jax.sharding import PartitionSpec as P

TOKENS = 256
HEADS = 32
WIDTH = 64
DSTATE = 256
REPEATS = 8
DIM = 128
META = 16
ROWS = TOKENS + META
HALF = HEADS * WIDTH // 2
QUARTER = HALF // 4
CHUNK = 2 * TOKENS
BLOCKS = 32
LEAD = 3

f32 = jnp.float32
bf16 = jnp.bfloat16
highest = lax.Precision.HIGHEST
negative = -1e30


def context_place():
    position = lax.axis_index("context")
    return position // 8, (position // 2) % 4, position % 2


def run(kernel, name, outs, *args, far=(), scratch=(), mib=16, flops=0, transcendentals=0):
    moved = sum(math.prod(a.shape) * a.dtype.itemsize for a in args)
    moved += sum(math.prod(a.shape) * a.dtype.itemsize for a in outs)
    spaces = [pltpu.HBM if number in far else pltpu.VMEM for number in range(len(args))]
    return pl.pallas_call(
        kernel,
        out_shape=outs,
        in_specs=[pl.BlockSpec(memory_space=space) for space in spaces],
        out_specs=[pl.BlockSpec(memory_space=pltpu.VMEM)] * len(outs),
        scratch_shapes=list(scratch),
        compiler_params=pltpu.CompilerParams(vmem_limit_bytes=mib << 20),
        cost_estimate=pl.CostEstimate(
            flops=flops, bytes_accessed=moved, transcendentals=transcendentals
        ),
        name=name,
    )(*args)


def shape(rows, columns, dtype=bf16):
    return jax.ShapeDtypeStruct((rows, columns), dtype)


def iota(rows, columns, axis):
    return lax.broadcasted_iota(jnp.int32, (rows, columns), axis)


def split3(value):
    high = value.astype(bf16)
    rest = value - high.astype(f32)
    middle = rest.astype(bf16)
    low = (rest - middle.astype(f32)).astype(bf16)
    return high, middle, low


def spread_matrix(chunk):
    column = iota(HEADS, 256, 1) + 256 * chunk
    return (column // WIDTH == iota(HEADS, 256, 0)).astype(bf16)


def spread(value, matrix):
    high, middle, _ = split3(value)
    return jnp.dot(high, matrix, preferred_element_type=f32) + jnp.dot(
        middle, matrix, preferred_element_type=f32
    )


def document_column(docs_row):
    return jnp.broadcast_to(docs_row.astype(f32), (128, TOKENS)).T


def fetch(sources, targets, semaphores):
    copies = [
        pltpu.make_async_copy(source, target, semaphores.at[number])
        for number, (source, target) in enumerate(zip(sources, targets))
    ]
    for copy in copies:
        copy.start()
    return copies


def write_kernel(*refs):
    far, (mine, theirs, cum_out, offset_out), held, semaphores = refs[:6], refs[6:10], refs[10:16], refs[16]
    copies = fetch(far, held, semaphores)
    raw, bias, decay, docs, inputs, writes = held
    _, _, core = context_place()
    for copy in copies[:4]:
        copy.wait()
    padded = jnp.concatenate([raw[...], jnp.zeros((128 - HEADS, TOKENS), f32)], axis=0)
    u = padded.T[:, :HEADS] + bias[...]
    step = jnp.maximum(u, 0.0) + jnp.log1p(jnp.exp(-jnp.abs(u)))
    logdec = -step * jnp.exp(decay[...])
    triangle = (iota(TOKENS, TOKENS, 0) >= iota(TOKENS, TOKENS, 1)).astype(f32)
    cum = jnp.dot(triangle, logdec, precision=highest, preferred_element_type=f32)
    cum_out[...] = cum
    offset = cum - jnp.log(step)
    padded = jnp.concatenate([offset, jnp.zeros((TOKENS, 128 - HEADS), f32)], axis=1)
    offset_out[...] = padded.T[:HEADS]
    total = cum[TOKENS - 1 :]
    column = document_column(docs[...])[:, :HEADS]
    last = column[TOKENS - 1 :]
    trail = jnp.where(column == last, jnp.exp(total - cum), 0.0) * step
    high, middle, low = [part.astype(f32) for part in split3(total)]
    row = iota(META, HEADS, 0)
    meta = jnp.where(
        row == 0,
        high,
        jnp.where(row == 1, middle, jnp.where(row == 2, low, jnp.where(row == 3, last, 0.0))),
    ).astype(bf16)
    copies[5].wait()
    turned = writes[...].T
    copies[4].wait()
    matrices = [spread_matrix(chunk) for chunk in range(8)]
    wide = [spread(trail, matrix) for matrix in matrices]
    scaled = [
        (inputs[:, 256 * chunk : 256 * (chunk + 1)].astype(f32) * wide[chunk]).astype(bf16)
        for chunk in range(8)
    ]
    states = [
        jnp.dot(turned, part, preferred_element_type=f32).astype(bf16) for part in scaled
    ]
    notes = [
        jnp.dot(meta, matrix, preferred_element_type=f32).astype(bf16) for matrix in matrices
    ]
    for chunk in range(4):
        columns = slice(256 * chunk, 256 * (chunk + 1))
        for rows, parts in ((slice(0, TOKENS), states), (slice(TOKENS, ROWS), notes)):
            mine[rows, columns] = jnp.where(core == 0, parts[chunk], parts[chunk + 4])
            theirs[rows, columns] = jnp.where(core == 0, parts[chunk + 4], parts[chunk])


def inside_kernel(cum, offset, docs, inputs, writes, reads, gain, out):
    scores = lax.dot_general(
        reads[...], writes[...], (((1,), (1,)), ((), ())), preferred_element_type=f32
    )
    column = document_column(docs[...])
    column = jnp.concatenate([column, column], axis=1)
    linked = (column == docs[...].astype(f32)) & (
        iota(TOKENS, TOKENS, 0) >= iota(TOKENS, TOKENS, 1)
    )
    scores = jnp.where(linked, scores, 0.0)
    upper = scores[:128, :128]
    lower = scores[128:]
    left = iota(TOKENS, 128, 1) < WIDTH
    for pair in range(HEADS // 2):
        columns = slice(128 * pair, 128 * (pair + 1))
        u = inputs[:, columns]
        zero = jnp.zeros_like(u)
        top = bottom = None
        for side in range(2):
            head = 2 * pair + side
            part = jnp.where(left, u, zero) if side == 0 else jnp.where(left, zero, u)
            ci = cum[:, head : head + 1]
            cj = offset[head : head + 1, :]
            first = (jnp.exp(ci[:128] - cj[:, :128]) * upper).astype(bf16)
            second = (jnp.exp(ci[128:] - cj) * lower).astype(bf16)
            first = jnp.dot(first, part[:128], preferred_element_type=f32)
            second = jnp.dot(second, part, preferred_element_type=f32)
            top = first if top is None else top + first
            bottom = second if bottom is None else bottom + second
        gains = jnp.where(
            left[:1], gain[:, 2 * pair : 2 * pair + 1], gain[:, 2 * pair + 1 : 2 * pair + 2]
        )
        wide = u.astype(f32) * gains
        out[:128, columns] = top + wide[:128]
        out[128:, columns] = bottom + wide[128:]


def described(ref_rows):
    rows = ref_rows.astype(f32)
    return rows[0:1] + rows[1:2] + rows[2:3], rows[3:4]


def meta_rows(total, last):
    high, middle, low = [part.astype(f32) for part in split3(total)]
    row = iota(META, total.shape[1], 0)
    return jnp.where(
        row == 0,
        high,
        jnp.where(row == 1, middle, jnp.where(row == 2, low, jnp.where(row == 3, last, 0.0))),
    ).astype(bf16)


def joined(earlier, later):
    total = earlier[1] + later[1]
    keep = jnp.where(later[2] == earlier[2], jnp.exp(later[1]), 0.0)
    return keep * earlier[0] + later[0], total, later[2]


def unpacked(payload):
    total, last = described(payload[TOKENS:])
    return payload[:TOKENS].astype(f32), total, last


def chip_kernel(mine, other, *outs):
    _, z, core = context_place()
    for step in range(4):
        columns = pl.ds(pl.multiple_of(((z + step) % 4) * QUARTER, QUARTER), QUARTER)
        own, near = mine[:, columns], other[:, columns]
        first = unpacked(jnp.where(core == 0, own, near))
        second = unpacked(jnp.where(core == 0, near, own))
        state, total, last = joined(first, second)
        outs[step][:TOKENS] = state.astype(bf16)
        outs[step][TOKENS:] = meta_rows(total, last)


def picked(slots, index):
    value = slots[0]
    for number in range(1, len(slots)):
        value = jnp.where(index == number, slots[number], value)
    return value


def row_kernel(a0, a1, a2, a3, out):
    _, z, _ = context_place()
    slots = [ref[...] for ref in (a0, a1, a2, a3)]
    whole = unpacked(picked(slots, z))
    for chip in range(1, 4):
        whole = joined(whole, unpacked(picked(slots, (z - chip) % 4)))
    out[:TOKENS] = whole[0].astype(bf16)
    out[TOKENS:] = meta_rows(whole[1], whole[2])


def entering_kernel(a0, a1, a2, a3, near, far, *outs):
    _, z, _ = context_place()
    slots = [ref[...] for ref in (a0, a1, a2, a3)]
    current = joined(unpacked(far[...]), unpacked(near[...]))
    entering = []
    for chip in range(4):
        entering.append((current[0].astype(bf16), meta_rows(current[1], current[2])))
        if chip < 3:
            current = joined(current, unpacked(picked(slots, (z - chip) % 4)))
    for step in range(4):
        outs[step][:TOKENS] = picked([e[0] for e in entering], (z + step) % 4)
        outs[step][TOKENS:] = picked([e[1] for e in entering], (z + step) % 4)


def core_kernel(b0, b1, b2, b3, mine, other, keep, send):
    _, z, core = context_place()
    for step, ref in enumerate((b0, b1, b2, b3)):
        columns = pl.ds(pl.multiple_of(((z - step) % 4) * QUARTER, QUARTER), QUARTER)
        first = ref[...]
        written = unpacked(jnp.where(core == 0, mine[:, columns], other[:, columns]))
        state, total, last = joined(unpacked(first), written)
        second = jnp.concatenate([state.astype(bf16), meta_rows(total, last)], axis=0)
        keep[:, columns] = jnp.where(core == 0, first, second)
        send[:, columns] = jnp.where(core == 0, second, first)


def carried_kernel(inside, cum, docs, reads, keep, other, out):
    _, _, core = context_place()
    before = keep[TOKENS:, :HEADS][3:4].astype(f32)
    column = document_column(docs[...])[:, :HEADS]
    factor = jnp.where(column == before, jnp.exp(cum[...]), 0.0)
    halves = [jnp.where(core == 0, keep[:TOKENS], other[:TOKENS])]
    halves.append(jnp.where(core == 0, other[:TOKENS], keep[:TOKENS]))
    carried = [
        jnp.dot(
            reads[...],
            halves[chunk // 4][:, 256 * (chunk % 4) : 256 * (chunk % 4 + 1)],
            preferred_element_type=f32,
        )
        for chunk in range(8)
    ]
    scale = [spread(factor, spread_matrix(chunk)) for chunk in range(8)]
    for chunk in range(8):
        columns = slice(256 * chunk, 256 * (chunk + 1))
        out[:, columns] = (inside[:, columns] + carried[chunk] * scale[chunk]).astype(bf16)


def cut_kernel(keys, values, *refs):
    outs, semaphores = refs[:4], refs[4]
    x = lax.axis_index("tensor")
    sources, targets = [], []
    for step in range(4):
        columns = pl.ds(pl.multiple_of(((x + step) % 4) * DIM, DIM), DIM)
        sources += [keys.at[:, columns], values.at[:, columns]]
        targets += [outs[step].at[:, :DIM], outs[step].at[:, DIM:]]
    for copy in fetch(sources, targets, semaphores):
        copy.wait()


def assemble_kernel(p0, p1, p2, p3, docs, out):
    x = lax.axis_index("tensor")
    for step, ref in enumerate((p0, p1, p2, p3)):
        out[pl.ds(pl.multiple_of(((x - step) % 4) * 64, 64), 64), :] = ref[...]
    first = jnp.sum(jnp.where(docs[...] >= 1, 1.0, 0.0), axis=1, keepdims=True)
    second = jnp.sum(jnp.where(docs[...] >= 2, 1.0, 0.0), axis=1, keepdims=True)
    lane = iota(META, 2 * DIM, 1)
    counts = jnp.where(lane == 1, first, jnp.where(lane == 2, second, 0.0))
    out[TOKENS:] = jnp.where(lane == 0, float(TOKENS), counts).astype(bf16)


def chunk_kernel(mine, other, out):
    _, _, core = context_place()
    out[:ROWS] = jnp.where(core == 0, mine[...], other[...])
    out[ROWS:] = jnp.where(core == 0, other[...], mine[...])


def far_kernel(chunk, above, *outs):
    _, z, core = context_place()
    for step in range(1, 4):
        own = (core == 1) & ((z + step) % 4 > z)
        outs[step - 1][...] = jnp.where(own, chunk[...], above[...])


def bundle_kernel(a0, a1, a2, a3, out):
    for step, ref in enumerate((a0, a1, a2, a3)):
        out[2 * ROWS * step : 2 * ROWS * (step + 1)] = ref[...]


def attention_kernel(queries, docs, chunk_ref, bundle, arrived, out, turned, peaks, sums):
    y, z, core = context_place()
    base = lax.axis_index("context") * TOKENS
    own = y * 4 + z
    ids = docs[...]
    opening = jnp.min(ids)
    counts = jnp.where(core == 1, chunk_ref[TOKENS:ROWS, :128].astype(f32), 0.0)
    for block in range(8):
        rows = slice(block * ROWS + TOKENS, (block + 1) * ROWS)
        counts = counts + bundle[rows, :128].astype(f32) + arrived[rows, :128].astype(f32)
    here = (iota(META, 128, 0) == 0) & (iota(META, 128, 1) == opening)
    start = base - jnp.sum(jnp.where(here, counts, 0.0)).astype(jnp.int32)
    below_two = jnp.sum(jnp.where(ids < 2, 1.0, 0.0)).astype(jnp.int32)
    below_one = jnp.sum(jnp.where(ids < 1, 1.0, 0.0)).astype(jnp.int32)
    lowest = jnp.where(ids == opening, start, base + jnp.where(ids == 1, below_one, below_two))
    highest_start = jnp.max(lowest)
    token = base + iota(1, TOKENS, 1)

    factor = math.log2(math.e) / math.sqrt(DIM)
    for head in range(REPEATS):
        scaled = (queries[:, head * DIM : (head + 1) * DIM].astype(f32) * factor).T
        high, middle, _ = split3(scaled)
        turned[head, :DIM] = high
        turned[head, DIM:] = middle
    peaks[...] = jnp.full_like(peaks, negative)
    sums[...] = jnp.zeros_like(sums)

    def rows_of(chunk, masked):
        near = chunk // 4 == y - 1
        slot = ((z - chunk) % 4) * 2 * ROWS
        found = []
        for block in range(2):
            place = pl.ds(pl.multiple_of(slot + block * ROWS, ROWS), TOKENS)
            rows = jnp.where(near == (core == 0), bundle[place, :], arrived[place, :])
            if masked:
                rows = jnp.where(chunk == own, chunk_ref[block * ROWS : block * ROWS + TOKENS], rows)
            found.append(rows)
        return found

    def fold(chunk, masked):
        one, two = rows_of(chunk, masked)
        keys = jnp.concatenate([one[:, :DIM], two[:, :DIM]], axis=0)
        keys = jnp.concatenate([keys, keys], axis=1)
        values = jnp.concatenate([one[:, DIM:], two[:, DIM:]], axis=0)
        values = jnp.concatenate([values.T, jnp.ones((META, CHUNK), bf16)], axis=0)
        if masked:
            place = chunk * CHUNK + iota(CHUNK, TOKENS, 0)
            allowed = (place <= token) & (place >= lowest)
            bias = jnp.where(allowed, 0.0, negative)

        def score(head):
            scores = jnp.dot(keys, turned[head], preferred_element_type=f32)
            return scores + bias if masked else scores

        def add(head, weights, shrink):
            sums[head] = sums[head] * shrink + jnp.dot(
                values, weights, preferred_element_type=f32
            )

        ahead = [score(head) for head in range(LEAD)]
        pending = None
        for head in range(REPEATS):
            if head + LEAD < REPEATS:
                ahead.append(score(head + LEAD))
            scores = ahead[head]
            old = peaks[head : head + 1]
            new = jnp.maximum(old, jnp.max(scores, axis=0, keepdims=True))
            weights = jnp.exp2(scores - new).astype(bf16)
            peaks[head : head + 1] = new
            if pending is not None:
                add(*pending)
            pending = (head, weights, jnp.exp2(old - new))
        add(*pending)

    first = start // CHUNK
    clear = jnp.minimum((highest_start + CHUNK - 1) // CHUNK, own)
    edges = clear - first

    @pl.loop(0, edges + 1)
    def _(number):
        fold(jnp.where(number < edges, first + number, own), True)

    @pl.loop(clear, own)
    def _(chunk):
        fold(chunk, False)

    for head in range(REPEATS):
        result = sums[head, :DIM] * (1.0 / sums[head, DIM : DIM + 1])
        out[:, head * DIM : (head + 1) * DIM] = result.T.astype(bf16)


def around_z(steps):
    return [
        (y * 8 + z * 2 + k, y * 8 + ((z + steps) % 4) * 2 + k)
        for y in range(4)
        for z in range(4)
        for k in range(2)
    ]


def along_y(steps):
    return [(c, c + 8 * steps) for c in range(BLOCKS - 8 * steps)]


def body(
    mixer_input,
    step_raw,
    step_bias,
    decay_log,
    skip_gain,
    write_keys,
    read_keys,
    document_ids,
    query_rows,
    key_rows,
    value_rows,
):
    docs = document_ids.reshape(1, TOKENS)
    across = [(c, c ^ 1) for c in range(BLOCKS)]
    below = [(c, c + 8 * (1 + c % 2)) for c in range(BLOCKS) if c + 8 * (1 + c % 2) < BLOCKS]

    cuts = run(
        cut_kernel,
        "cut_keys",
        [shape(64, 2 * DIM)] * 4,
        key_rows,
        value_rows,
        far=(0, 1),
        scratch=[pltpu.SemaphoreType.DMA((8,))],
        mib=56,
    )
    parts = [cuts[0]] + [
        lax.ppermute(cuts[step], "tensor", [(x, (x + step) % 4) for x in range(4)])
        for step in (1, 2, 3)
    ]

    mine, theirs, cum, offset = run(
        write_kernel,
        "mixer_write",
        [shape(ROWS, HALF), shape(ROWS, HALF), shape(TOKENS, HEADS, f32), shape(HEADS, TOKENS, f32)],
        step_raw.T,
        step_bias.reshape(1, HEADS),
        decay_log.reshape(1, HEADS),
        docs,
        mixer_input,
        write_keys,
        far=range(6),
        scratch=[
            pltpu.VMEM((HEADS, TOKENS), f32),
            pltpu.VMEM((1, HEADS), f32),
            pltpu.VMEM((1, HEADS), f32),
            pltpu.VMEM((1, TOKENS), jnp.int32),
            pltpu.VMEM((TOKENS, HEADS * WIDTH), bf16),
            pltpu.VMEM((TOKENS, DSTATE), bf16),
            pltpu.SemaphoreType.DMA((6,)),
        ],
        mib=56,
        flops=2 * 256 * 256 * 2048,
    )
    parts, mine, theirs, cum, offset = lax.optimization_barrier((parts, mine, theirs, cum, offset))
    (block,) = run(assemble_kernel, "assemble_keys", [shape(ROWS, 2 * DIM)], *parts, docs)
    other_block = lax.ppermute(block, "context", across)
    other = lax.ppermute(theirs, "context", across)

    other_block, other = lax.optimization_barrier((other_block, other))
    quarter = [shape(ROWS, QUARTER)]
    (chunk,) = run(chunk_kernel, "chunk_keys", [shape(2 * ROWS, 2 * DIM)], block, other_block)
    chips = run(chip_kernel, "chip_state", quarter * 4, mine, other)
    chunk, chips = lax.optimization_barrier((chunk, chips))
    above = lax.ppermute(chunk, "context", below)
    slots = [chips[0]] + [lax.ppermute(chips[s], "context", around_z(s)) for s in (1, 2, 3)]

    (inside,) = run(
        inside_kernel,
        "mixer_inside",
        [shape(TOKENS, HEADS * WIDTH, f32)],
        cum,
        offset,
        docs,
        mixer_input,
        write_keys,
        read_keys,
        skip_gain.reshape(1, HEADS),
        mib=24,
        flops=2 * 256 * 256 * 128 * 32,
    )

    above, inside = lax.optimization_barrier((above, inside))
    far_cuts = run(far_kernel, "far_keys", [shape(2 * ROWS, 2 * DIM)] * 3, chunk, above)
    far = [lax.ppermute(far_cuts[s - 1], "context", around_z(s)) for s in (1, 2, 3)]

    slots, far_cuts = lax.optimization_barrier((slots, far_cuts))
    (row,) = run(row_kernel, "row_state", quarter, *slots)
    near_row = lax.ppermute(row, "context", along_y(1))
    far_row = lax.ppermute(row, "context", along_y(2))
    entering = run(entering_kernel, "entering_state", quarter * 4, *slots, near_row, far_row)
    back = [entering[0]] + [lax.ppermute(entering[s], "context", around_z(s)) for s in (1, 2, 3)]

    far, entering = lax.optimization_barrier((far, entering))
    (bundle,) = run(bundle_kernel, "bundle_keys", [shape(8 * ROWS, 2 * DIM)], above, *far)
    arrived = lax.ppermute(bundle, "context", across)

    (attended,) = run(
        attention_kernel,
        "attention",
        [shape(TOKENS, REPEATS * DIM)],
        query_rows,
        docs,
        chunk,
        bundle,
        arrived,
        scratch=[
            pltpu.VMEM((REPEATS, 2 * DIM, TOKENS), bf16),
            pltpu.VMEM((REPEATS, TOKENS), f32),
            pltpu.VMEM((REPEATS, DIM + META, TOKENS), f32),
        ],
        mib=32,
        flops=4 * 2048 * 4096 * 128,
        transcendentals=2048 * 4096,
    )

    keep, send = run(core_kernel, "core_state", [shape(ROWS, HALF)] * 2, *back, mine, other)
    state_arrived = lax.ppermute(send, "context", across)
    (mixed,) = run(
        carried_kernel,
        "mixer_carried",
        [shape(TOKENS, HEADS * WIDTH)],
        inside,
        cum,
        docs,
        read_keys,
        keep,
        state_arrived,
        mib=24,
        flops=2 * 256 * 256 * 2048,
    )
    return mixed, attended


def solution(mesh):
    placed = (
        P("context", "tensor"),
        P("context", "tensor"),
        P("tensor"),
        P("tensor"),
        P("tensor"),
        P("context", "tensor"),
        P("context", "tensor"),
        P("context"),
        P("context", "tensor"),
        P(("context", "tensor"), None),
        P(("context", "tensor"), None),
    )
    return jax.shard_map(
        body,
        mesh=mesh,
        in_specs=placed,
        out_specs=(P("context", "tensor"), P("context", "tensor")),
        check_vma=False,
    )
```

```python
import math

import jax
import jax.numpy as jnp
from jax import lax
from jax.experimental import pallas as pl
from jax.experimental.pallas import tpu as pltpu
from jax.sharding import PartitionSpec as P

TOKENS = 256
HEADS = 32
WIDTH = 64
DSTATE = 256
REPEATS = 8
DIM = 128
META = 16
ROWS = TOKENS + META
HALF = HEADS * WIDTH // 2
QUARTER = HALF // 4
CHUNK = 2 * TOKENS
BLOCKS = 32
LEAD = 3

f32 = jnp.float32
bf16 = jnp.bfloat16
highest = lax.Precision.HIGHEST
negative = -1e30


def context_place():
    position = lax.axis_index("context")
    return position // 8, (position // 2) % 4, position % 2


def run(kernel, name, outs, *args, far=(), scratch=(), mib=16, flops=0, transcendentals=0):
    moved = sum(math.prod(a.shape) * a.dtype.itemsize for a in args)
    moved += sum(math.prod(a.shape) * a.dtype.itemsize for a in outs)
    spaces = [pltpu.HBM if number in far else pltpu.VMEM for number in range(len(args))]
    return pl.pallas_call(
        kernel,
        out_shape=outs,
        in_specs=[pl.BlockSpec(memory_space=space) for space in spaces],
        out_specs=[pl.BlockSpec(memory_space=pltpu.VMEM)] * len(outs),
        scratch_shapes=list(scratch),
        compiler_params=pltpu.CompilerParams(vmem_limit_bytes=mib << 20),
        cost_estimate=pl.CostEstimate(
            flops=flops, bytes_accessed=moved, transcendentals=transcendentals
        ),
        name=name,
    )(*args)


def shape(rows, columns, dtype=bf16):
    return jax.ShapeDtypeStruct((rows, columns), dtype)


def iota(rows, columns, axis):
    return lax.broadcasted_iota(jnp.int32, (rows, columns), axis)


def split3(value):
    high = value.astype(bf16)
    rest = value - high.astype(f32)
    middle = rest.astype(bf16)
    low = (rest - middle.astype(f32)).astype(bf16)
    return high, middle, low


def spread_matrix(chunk):
    column = iota(HEADS, 256, 1) + 256 * chunk
    return (column // WIDTH == iota(HEADS, 256, 0)).astype(bf16)


def spread(value, matrix):
    high, middle, _ = split3(value)
    return jnp.dot(high, matrix, preferred_element_type=f32) + jnp.dot(
        middle, matrix, preferred_element_type=f32
    )


def document_column(docs_row):
    return jnp.broadcast_to(docs_row.astype(f32), (128, TOKENS)).T


def fetch(sources, targets, semaphores):
    copies = [
        pltpu.make_async_copy(source, target, semaphores.at[number])
        for number, (source, target) in enumerate(zip(sources, targets))
    ]
    for copy in copies:
        copy.start()
    return copies


def write_kernel(*refs):
    far, (mine, theirs, cum_out, offset_out), held, semaphores = refs[:6], refs[6:10], refs[10:16], refs[16]
    copies = fetch(far, held, semaphores)
    raw, bias, decay, docs, inputs, writes = held
    _, _, core = context_place()
    for copy in copies[:4]:
        copy.wait()
    padded = jnp.concatenate([raw[...], jnp.zeros((128 - HEADS, TOKENS), f32)], axis=0)
    u = padded.T[:, :HEADS] + bias[...]
    step = jnp.maximum(u, 0.0) + jnp.log1p(jnp.exp(-jnp.abs(u)))
    logdec = -step * jnp.exp(decay[...])
    triangle = (iota(TOKENS, TOKENS, 0) >= iota(TOKENS, TOKENS, 1)).astype(f32)
    cum = jnp.dot(triangle, logdec, precision=highest, preferred_element_type=f32)
    cum_out[...] = cum
    offset = cum - jnp.log(step)
    padded = jnp.concatenate([offset, jnp.zeros((TOKENS, 128 - HEADS), f32)], axis=1)
    offset_out[...] = padded.T[:HEADS]
    total = cum[TOKENS - 1 :]
    column = document_column(docs[...])[:, :HEADS]
    last = column[TOKENS - 1 :]
    trail = jnp.where(column == last, jnp.exp(total - cum), 0.0) * step
    high, middle, low = [part.astype(f32) for part in split3(total)]
    row = iota(META, HEADS, 0)
    meta = jnp.where(
        row == 0,
        high,
        jnp.where(row == 1, middle, jnp.where(row == 2, low, jnp.where(row == 3, last, 0.0))),
    ).astype(bf16)
    copies[5].wait()
    turned = writes[...].T
    copies[4].wait()
    matrices = [spread_matrix(chunk) for chunk in range(8)]
    wide = [spread(trail, matrix) for matrix in matrices]
    scaled = [
        (inputs[:, 256 * chunk : 256 * (chunk + 1)].astype(f32) * wide[chunk]).astype(bf16)
        for chunk in range(8)
    ]
    states = [
        jnp.dot(turned, part, preferred_element_type=f32).astype(bf16) for part in scaled
    ]
    notes = [
        jnp.dot(meta, matrix, preferred_element_type=f32).astype(bf16) for matrix in matrices
    ]
    for chunk in range(4):
        columns = slice(256 * chunk, 256 * (chunk + 1))
        for rows, parts in ((slice(0, TOKENS), states), (slice(TOKENS, ROWS), notes)):
            mine[rows, columns] = jnp.where(core == 0, parts[chunk], parts[chunk + 4])
            theirs[rows, columns] = jnp.where(core == 0, parts[chunk + 4], parts[chunk])


def inside_kernel(cum, offset, docs, inputs, writes, reads, gain, out):
    scores = lax.dot_general(
        reads[...], writes[...], (((1,), (1,)), ((), ())), preferred_element_type=f32
    )
    column = document_column(docs[...])
    column = jnp.concatenate([column, column], axis=1)
    linked = (column == docs[...].astype(f32)) & (
        iota(TOKENS, TOKENS, 0) >= iota(TOKENS, TOKENS, 1)
    )
    scores = jnp.where(linked, scores, 0.0)
    upper = scores[:128, :128]
    lower = scores[128:]
    left = iota(TOKENS, 128, 1) < WIDTH
    for pair in range(HEADS // 2):
        columns = slice(128 * pair, 128 * (pair + 1))
        u = inputs[:, columns]
        zero = jnp.zeros_like(u)
        top = bottom = None
        for side in range(2):
            head = 2 * pair + side
            part = jnp.where(left, u, zero) if side == 0 else jnp.where(left, zero, u)
            ci = cum[:, head : head + 1]
            cj = offset[head : head + 1, :]
            first = (jnp.exp(ci[:128] - cj[:, :128]) * upper).astype(bf16)
            second = (jnp.exp(ci[128:] - cj) * lower).astype(bf16)
            first = jnp.dot(first, part[:128], preferred_element_type=f32)
            second = jnp.dot(second, part, preferred_element_type=f32)
            top = first if top is None else top + first
            bottom = second if bottom is None else bottom + second
        gains = jnp.where(
            left[:1], gain[:, 2 * pair : 2 * pair + 1], gain[:, 2 * pair + 1 : 2 * pair + 2]
        )
        wide = u.astype(f32) * gains
        out[:128, columns] = top + wide[:128]
        out[128:, columns] = bottom + wide[128:]


def described(ref_rows):
    rows = ref_rows.astype(f32)
    return rows[0:1] + rows[1:2] + rows[2:3], rows[3:4]


def meta_rows(total, last):
    high, middle, low = [part.astype(f32) for part in split3(total)]
    row = iota(META, total.shape[1], 0)
    return jnp.where(
        row == 0,
        high,
        jnp.where(row == 1, middle, jnp.where(row == 2, low, jnp.where(row == 3, last, 0.0))),
    ).astype(bf16)


def joined(earlier, later):
    total = earlier[1] + later[1]
    keep = jnp.where(later[2] == earlier[2], jnp.exp(later[1]), 0.0)
    return keep * earlier[0] + later[0], total, later[2]


def unpacked(payload):
    total, last = described(payload[TOKENS:])
    return payload[:TOKENS].astype(f32), total, last


def chip_kernel(mine, other, *outs):
    _, z, core = context_place()
    for step in range(4):
        columns = pl.ds(pl.multiple_of(((z + step) % 4) * QUARTER, QUARTER), QUARTER)
        own, near = mine[:, columns], other[:, columns]
        first = unpacked(jnp.where(core == 0, own, near))
        second = unpacked(jnp.where(core == 0, near, own))
        state, total, last = joined(first, second)
        outs[step][:TOKENS] = state.astype(bf16)
        outs[step][TOKENS:] = meta_rows(total, last)


def picked(slots, index):
    value = slots[0]
    for number in range(1, len(slots)):
        value = jnp.where(index == number, slots[number], value)
    return value


def row_kernel(a0, a1, a2, a3, out):
    _, z, _ = context_place()
    slots = [ref[...] for ref in (a0, a1, a2, a3)]
    whole = unpacked(picked(slots, z))
    for chip in range(1, 4):
        whole = joined(whole, unpacked(picked(slots, (z - chip) % 4)))
    out[:TOKENS] = whole[0].astype(bf16)
    out[TOKENS:] = meta_rows(whole[1], whole[2])


def entering_kernel(a0, a1, a2, a3, near, far, *outs):
    _, z, _ = context_place()
    slots = [ref[...] for ref in (a0, a1, a2, a3)]
    current = joined(unpacked(far[...]), unpacked(near[...]))
    entering = []
    for chip in range(4):
        entering.append((current[0].astype(bf16), meta_rows(current[1], current[2])))
        if chip < 3:
            current = joined(current, unpacked(picked(slots, (z - chip) % 4)))
    for step in range(4):
        outs[step][:TOKENS] = picked([e[0] for e in entering], (z + step) % 4)
        outs[step][TOKENS:] = picked([e[1] for e in entering], (z + step) % 4)


def core_kernel(b0, b1, b2, b3, mine, other, keep, send):
    _, z, core = context_place()
    for step, ref in enumerate((b0, b1, b2, b3)):
        columns = pl.ds(pl.multiple_of(((z - step) % 4) * QUARTER, QUARTER), QUARTER)
        first = ref[...]
        written = unpacked(jnp.where(core == 0, mine[:, columns], other[:, columns]))
        state, total, last = joined(unpacked(first), written)
        second = jnp.concatenate([state.astype(bf16), meta_rows(total, last)], axis=0)
        keep[:, columns] = jnp.where(core == 0, first, second)
        send[:, columns] = jnp.where(core == 0, second, first)


def carried_kernel(inside, cum, docs, reads, keep, other, out):
    _, _, core = context_place()
    before = keep[TOKENS:, :HEADS][3:4].astype(f32)
    column = document_column(docs[...])[:, :HEADS]
    factor = jnp.where(column == before, jnp.exp(cum[...]), 0.0)
    halves = [jnp.where(core == 0, keep[:TOKENS], other[:TOKENS])]
    halves.append(jnp.where(core == 0, other[:TOKENS], keep[:TOKENS]))
    carried = [
        jnp.dot(
            reads[...],
            halves[chunk // 4][:, 256 * (chunk % 4) : 256 * (chunk % 4 + 1)],
            preferred_element_type=f32,
        )
        for chunk in range(8)
    ]
    scale = [spread(factor, spread_matrix(chunk)) for chunk in range(8)]
    for chunk in range(8):
        columns = slice(256 * chunk, 256 * (chunk + 1))
        out[:, columns] = (inside[:, columns] + carried[chunk] * scale[chunk]).astype(bf16)


def cut_kernel(keys, values, *refs):
    outs, semaphores = refs[:4], refs[4]
    x = lax.axis_index("tensor")
    sources, targets = [], []
    for step in range(4):
        columns = pl.ds(pl.multiple_of(((x + step) % 4) * DIM, DIM), DIM)
        sources += [keys.at[:, columns], values.at[:, columns]]
        targets += [outs[step].at[:, :DIM], outs[step].at[:, DIM:]]
    for copy in fetch(sources, targets, semaphores):
        copy.wait()


def assemble_kernel(p0, p1, p2, p3, docs, out):
    x = lax.axis_index("tensor")
    for step, ref in enumerate((p0, p1, p2, p3)):
        out[pl.ds(pl.multiple_of(((x - step) % 4) * 64, 64), 64), :] = ref[...]
    first = jnp.sum(jnp.where(docs[...] >= 1, 1.0, 0.0), axis=1, keepdims=True)
    second = jnp.sum(jnp.where(docs[...] >= 2, 1.0, 0.0), axis=1, keepdims=True)
    lane = iota(META, 2 * DIM, 1)
    counts = jnp.where(lane == 1, first, jnp.where(lane == 2, second, 0.0))
    out[TOKENS:] = jnp.where(lane == 0, float(TOKENS), counts).astype(bf16)


def chunk_kernel(mine, other, out):
    _, _, core = context_place()
    out[:ROWS] = jnp.where(core == 0, mine[...], other[...])
    out[ROWS:] = jnp.where(core == 0, other[...], mine[...])


def far_kernel(chunk, above, *outs):
    _, z, core = context_place()
    for step in range(1, 4):
        own = (core == 1) & ((z + step) % 4 > z)
        outs[step - 1][...] = jnp.where(own, chunk[...], above[...])


def bundle_kernel(a0, a1, a2, a3, out):
    for step, ref in enumerate((a0, a1, a2, a3)):
        out[2 * ROWS * step : 2 * ROWS * (step + 1)] = ref[...]


def chunk_of(blocks):
    one, two = blocks
    keys = jnp.concatenate([one[:, :DIM], two[:, :DIM]], axis=0)
    values = jnp.concatenate([one[:, DIM:], two[:, DIM:]], axis=0)
    values = jnp.concatenate([values.T, jnp.ones((META, CHUNK), bf16)], axis=0)
    return jnp.concatenate([keys, keys], axis=1), values


def mask_of(chunk, token, lowest):
    place = chunk * CHUNK + iota(CHUNK, TOKENS, 0)
    return jnp.where((place <= token) & (place >= lowest), 0.0, negative)


def fold(keys, values, bias, turned, peaks, sums, first):
    def score(head):
        scores = jnp.dot(keys, turned[head], preferred_element_type=f32)
        return scores if bias is None else scores + bias

    def add(head, weights, shrink):
        new = jnp.dot(values, weights, preferred_element_type=f32)
        sums[head] = new if first else sums[head] * shrink + new

    ahead = [score(head) for head in range(LEAD)]
    pending = None
    for head in range(REPEATS):
        if head + LEAD < REPEATS:
            ahead.append(score(head + LEAD))
        scores = ahead[head]
        new = jnp.max(scores, axis=0, keepdims=True)
        shrink = None
        if not first:
            old = peaks[head : head + 1]
            new = jnp.maximum(old, new)
            shrink = jnp.exp2(old - new)
        weights = jnp.exp2(scores - new).astype(bf16)
        peaks[head : head + 1] = new
        if pending is not None:
            add(*pending)
        pending = (head, weights, shrink)
    add(*pending)


def starts_of(ids, start, base):
    below_one = jnp.sum(jnp.where(ids < 1, 1.0, 0.0)).astype(jnp.int32)
    below_two = jnp.sum(jnp.where(ids < 2, 1.0, 0.0)).astype(jnp.int32)
    opening = jnp.min(ids)
    return jnp.where(ids == opening, start, base + jnp.where(ids == 1, below_one, below_two))


def counted(counts, opening):
    here = (iota(META, 128, 0) == 0) & (iota(META, 128, 1) == opening)
    return jnp.sum(jnp.where(here, counts, 0.0)).astype(jnp.int32)


def own_kernel(queries, docs, chunk_ref, turned, peaks, sums):
    y, z, core = context_place()
    base = lax.axis_index("context") * TOKENS
    ids = docs[...]
    earlier = jnp.where(core == 1, chunk_ref[TOKENS:ROWS, :128].astype(f32), 0.0)
    lowest = starts_of(ids, base - counted(earlier, jnp.min(ids)), base)
    factor = math.log2(math.e) / math.sqrt(DIM)
    for head in range(REPEATS):
        scaled = (queries[:, head * DIM : (head + 1) * DIM].astype(f32) * factor).T
        high, middle, _ = split3(scaled)
        turned[head, :DIM] = high
        turned[head, DIM:] = middle
    bias = mask_of(y * 4 + z, base + iota(1, TOKENS, 1), lowest)
    keys, values = chunk_of([chunk_ref[:TOKENS], chunk_ref[ROWS : ROWS + TOKENS]])
    fold(keys, values, bias, turned, peaks, sums, True)


def attention_kernel(docs, chunk_ref, bundle, arrived, turned, own_peaks, own_sums, out, peaks, sums):
    y, z, core = context_place()
    base = lax.axis_index("context") * TOKENS
    own = y * 4 + z
    ids = docs[...]
    counts = jnp.where(core == 1, chunk_ref[TOKENS:ROWS, :128].astype(f32), 0.0)
    for block in range(8):
        rows = slice(block * ROWS + TOKENS, (block + 1) * ROWS)
        counts = counts + bundle[rows, :128].astype(f32) + arrived[rows, :128].astype(f32)
    start = base - counted(counts, jnp.min(ids))
    lowest = starts_of(ids, start, base)
    token = base + iota(1, TOKENS, 1)
    peaks[...] = own_peaks[...]
    sums[...] = own_sums[...]

    def visit(chunk, masked):
        near = chunk // 4 == y - 1
        slot = ((z - chunk) % 4) * 2 * ROWS
        blocks = []
        for block in range(2):
            place = pl.ds(pl.multiple_of(slot + block * ROWS, ROWS), TOKENS)
            blocks.append(jnp.where(near == (core == 0), bundle[place, :], arrived[place, :]))
        keys, values = chunk_of(blocks)
        bias = mask_of(chunk, token, lowest) if masked else None
        fold(keys, values, bias, turned, peaks, sums, False)

    first = start // CHUNK
    clear = jnp.minimum((jnp.max(lowest) + CHUNK - 1) // CHUNK, own)

    @pl.loop(first, clear)
    def _(chunk):
        visit(chunk, True)

    @pl.loop(clear, own)
    def _(chunk):
        visit(chunk, False)

    for head in range(REPEATS):
        result = sums[head, :DIM] * (1.0 / sums[head, DIM : DIM + 1])
        out[:, head * DIM : (head + 1) * DIM] = result.T.astype(bf16)


def around_z(steps):
    return [
        (y * 8 + z * 2 + k, y * 8 + ((z + steps) % 4) * 2 + k)
        for y in range(4)
        for z in range(4)
        for k in range(2)
    ]


def along_y(steps):
    return [(c, c + 8 * steps) for c in range(BLOCKS - 8 * steps)]


def body(
    mixer_input,
    step_raw,
    step_bias,
    decay_log,
    skip_gain,
    write_keys,
    read_keys,
    document_ids,
    query_rows,
    key_rows,
    value_rows,
):
    docs = document_ids.reshape(1, TOKENS)
    across = [(c, c ^ 1) for c in range(BLOCKS)]
    below = [(c, c + 8 * (1 + c % 2)) for c in range(BLOCKS) if c + 8 * (1 + c % 2) < BLOCKS]

    cuts = run(
        cut_kernel,
        "cut_keys",
        [shape(64, 2 * DIM)] * 4,
        key_rows,
        value_rows,
        far=(0, 1),
        scratch=[pltpu.SemaphoreType.DMA((8,))],
        mib=56,
    )
    parts = [cuts[0]] + [
        lax.ppermute(cuts[step], "tensor", [(x, (x + step) % 4) for x in range(4)])
        for step in (1, 2, 3)
    ]

    mine, theirs, cum, offset = run(
        write_kernel,
        "mixer_write",
        [shape(ROWS, HALF), shape(ROWS, HALF), shape(TOKENS, HEADS, f32), shape(HEADS, TOKENS, f32)],
        step_raw.T,
        step_bias.reshape(1, HEADS),
        decay_log.reshape(1, HEADS),
        docs,
        mixer_input,
        write_keys,
        far=range(6),
        scratch=[
            pltpu.VMEM((HEADS, TOKENS), f32),
            pltpu.VMEM((1, HEADS), f32),
            pltpu.VMEM((1, HEADS), f32),
            pltpu.VMEM((1, TOKENS), jnp.int32),
            pltpu.VMEM((TOKENS, HEADS * WIDTH), bf16),
            pltpu.VMEM((TOKENS, DSTATE), bf16),
            pltpu.SemaphoreType.DMA((6,)),
        ],
        mib=56,
        flops=2 * 256 * 256 * 2048,
    )
    parts, mine, theirs, cum, offset = lax.optimization_barrier((parts, mine, theirs, cum, offset))
    (block,) = run(assemble_kernel, "assemble_keys", [shape(ROWS, 2 * DIM)], *parts, docs)
    other_block = lax.ppermute(block, "context", across)
    other = lax.ppermute(theirs, "context", across)

    other_block, other = lax.optimization_barrier((other_block, other))
    quarter = [shape(ROWS, QUARTER)]
    (chunk,) = run(chunk_kernel, "chunk_keys", [shape(2 * ROWS, 2 * DIM)], block, other_block)
    chips = run(chip_kernel, "chip_state", quarter * 4, mine, other)
    chunk, chips = lax.optimization_barrier((chunk, chips))
    above = lax.ppermute(chunk, "context", below)
    slots = [chips[0]] + [lax.ppermute(chips[s], "context", around_z(s)) for s in (1, 2, 3)]

    (inside,) = run(
        inside_kernel,
        "mixer_inside",
        [shape(TOKENS, HEADS * WIDTH, f32)],
        cum,
        offset,
        docs,
        mixer_input,
        write_keys,
        read_keys,
        skip_gain.reshape(1, HEADS),
        mib=24,
        flops=2 * 256 * 256 * 128 * 32,
    )

    above, inside = lax.optimization_barrier((above, inside))
    far_cuts = run(far_kernel, "far_keys", [shape(2 * ROWS, 2 * DIM)] * 3, chunk, above)
    far = [lax.ppermute(far_cuts[s - 1], "context", around_z(s)) for s in (1, 2, 3)]

    slots, far_cuts = lax.optimization_barrier((slots, far_cuts))
    (row,) = run(row_kernel, "row_state", quarter, *slots)
    near_row = lax.ppermute(row, "context", along_y(1))
    far_row = lax.ppermute(row, "context", along_y(2))
    turned, peaks, sums = run(
        own_kernel,
        "attention_own",
        [
            jax.ShapeDtypeStruct((REPEATS, 2 * DIM, TOKENS), bf16),
            shape(REPEATS, TOKENS, f32),
            jax.ShapeDtypeStruct((REPEATS, DIM + META, TOKENS), f32),
        ],
        query_rows,
        docs,
        chunk,
        mib=24,
        flops=4 * 2048 * 512 * 128,
        transcendentals=2048 * 512,
    )
    near_row, far_row, turned = lax.optimization_barrier((near_row, far_row, turned))
    entering = run(entering_kernel, "entering_state", quarter * 4, *slots, near_row, far_row)
    back = [entering[0]] + [lax.ppermute(entering[s], "context", around_z(s)) for s in (1, 2, 3)]

    far, entering = lax.optimization_barrier((far, entering))
    (bundle,) = run(bundle_kernel, "bundle_keys", [shape(8 * ROWS, 2 * DIM)], above, *far)
    arrived = lax.ppermute(bundle, "context", across)

    (attended,) = run(
        attention_kernel,
        "attention",
        [shape(TOKENS, REPEATS * DIM)],
        docs,
        chunk,
        bundle,
        arrived,
        turned,
        peaks,
        sums,
        scratch=[
            pltpu.VMEM((REPEATS, TOKENS), f32),
            pltpu.VMEM((REPEATS, DIM + META, TOKENS), f32),
        ],
        mib=32,
        flops=4 * 2048 * 4096 * 128,
        transcendentals=2048 * 4096,
    )
    back, attended = lax.optimization_barrier((back, attended))

    keep, send = run(core_kernel, "core_state", [shape(ROWS, HALF)] * 2, *back, mine, other)
    state_arrived = lax.ppermute(send, "context", across)
    (mixed,) = run(
        carried_kernel,
        "mixer_carried",
        [shape(TOKENS, HEADS * WIDTH)],
        inside,
        cum,
        docs,
        read_keys,
        keep,
        state_arrived,
        mib=24,
        flops=2 * 256 * 256 * 2048,
    )
    return mixed, attended


def solution(mesh):
    placed = (
        P("context", "tensor"),
        P("context", "tensor"),
        P("tensor"),
        P("tensor"),
        P("tensor"),
        P("context", "tensor"),
        P("context", "tensor"),
        P("context"),
        P("context", "tensor"),
        P(("context", "tensor"), None),
        P(("context", "tensor"), None),
    )
    return jax.shard_map(
        body,
        mesh=mesh,
        in_specs=placed,
        out_specs=(P("context", "tensor"), P("context", "tensor")),
        check_vma=False,
    )
```

```python
import math

import jax
import jax.numpy as jnp
from jax import lax
from jax.experimental import pallas as pl
from jax.experimental.pallas import tpu as pltpu
from jax.sharding import PartitionSpec as P

TOKENS = 256
HEADS = 32
WIDTH = 64
DSTATE = 256
REPEATS = 8
DIM = 128
META = 16
ROWS = TOKENS + META
HALF = HEADS * WIDTH // 2
QUARTER = HALF // 4
CHUNK = 2 * TOKENS
BLOCKS = 32
LEAD = 3

f32 = jnp.float32
bf16 = jnp.bfloat16
highest = lax.Precision.HIGHEST
negative = -1e30


def context_place():
    position = lax.axis_index("context")
    return position // 8, (position // 2) % 4, position % 2


def run(kernel, name, outs, *args, far=(), scratch=(), mib=16, flops=0, transcendentals=0):
    moved = sum(math.prod(a.shape) * a.dtype.itemsize for a in args)
    moved += sum(math.prod(a.shape) * a.dtype.itemsize for a in outs)
    spaces = [pltpu.HBM if number in far else pltpu.VMEM for number in range(len(args))]
    return pl.pallas_call(
        kernel,
        out_shape=outs,
        in_specs=[pl.BlockSpec(memory_space=space) for space in spaces],
        out_specs=[pl.BlockSpec(memory_space=pltpu.VMEM)] * len(outs),
        scratch_shapes=list(scratch),
        compiler_params=pltpu.CompilerParams(vmem_limit_bytes=mib << 20),
        cost_estimate=pl.CostEstimate(
            flops=flops, bytes_accessed=moved, transcendentals=transcendentals
        ),
        name=name,
    )(*args)


def shape(rows, columns, dtype=bf16):
    return jax.ShapeDtypeStruct((rows, columns), dtype)


def iota(rows, columns, axis):
    return lax.broadcasted_iota(jnp.int32, (rows, columns), axis)


def split3(value):
    high = value.astype(bf16)
    rest = value - high.astype(f32)
    middle = rest.astype(bf16)
    low = (rest - middle.astype(f32)).astype(bf16)
    return high, middle, low


def spread_matrix(chunk):
    column = iota(2 * HEADS, 256, 1) + 256 * chunk
    return (column // WIDTH == iota(2 * HEADS, 256, 0) % HEADS).astype(bf16)


def two_parts(value):
    high, middle, _ = split3(value)
    return jnp.concatenate([high, middle], axis=1)


def spread(parts, matrix):
    return jnp.dot(parts, matrix, preferred_element_type=f32)


def document_column(docs_row):
    return jnp.broadcast_to(docs_row.astype(f32), (128, TOKENS)).T


def fetch(sources, targets, semaphores):
    copies = [
        pltpu.make_async_copy(source, target, semaphores.at[number])
        for number, (source, target) in enumerate(zip(sources, targets))
    ]
    for copy in copies:
        copy.start()
    return copies


def write_kernel(*refs):
    far, (mine, theirs, cum_out, offset_out), held, semaphores = refs[:6], refs[6:10], refs[10:16], refs[16]
    copies = fetch(far, held, semaphores)
    raw, bias, decay, docs, inputs, writes = held
    _, _, core = context_place()
    for copy in copies[:4]:
        copy.wait()
    padded = jnp.concatenate([raw[...], jnp.zeros((128 - HEADS, TOKENS), f32)], axis=0)
    u = padded.T[:, :HEADS] + bias[...]
    step = jnp.maximum(u, 0.0) + jnp.log1p(jnp.exp(-jnp.abs(u)))
    logdec = -step * jnp.exp(decay[...])
    triangle = (iota(TOKENS, TOKENS, 0) >= iota(TOKENS, TOKENS, 1)).astype(f32)
    cum = jnp.dot(triangle, logdec, precision=highest, preferred_element_type=f32)
    cum_out[...] = cum
    offset = cum - jnp.log(step)
    padded = jnp.concatenate([offset, jnp.zeros((TOKENS, 128 - HEADS), f32)], axis=1)
    offset_out[...] = padded.T[:HEADS]
    total = cum[TOKENS - 1 :]
    column = document_column(docs[...])[:, :HEADS]
    last = column[TOKENS - 1 :]
    trail = jnp.where(column == last, jnp.exp(total - cum), 0.0) * step
    high, middle, low = [part.astype(f32) for part in split3(total)]
    row = iota(META, HEADS, 0)
    meta = jnp.where(
        row == 0,
        high,
        jnp.where(row == 1, middle, jnp.where(row == 2, low, jnp.where(row == 3, last, 0.0))),
    ).astype(bf16)
    copies[5].wait()
    turned = writes[...].T
    copies[4].wait()
    matrices = [spread_matrix(chunk) for chunk in range(8)]
    trail = two_parts(trail)
    wide = [spread(trail, matrix) for matrix in matrices]
    scaled = [
        (inputs[:, 256 * chunk : 256 * (chunk + 1)].astype(f32) * wide[chunk]).astype(bf16)
        for chunk in range(8)
    ]
    states = [
        jnp.dot(turned, part, preferred_element_type=f32).astype(bf16) for part in scaled
    ]
    notes = [
        jnp.dot(meta, matrix[:HEADS], preferred_element_type=f32).astype(bf16) for matrix in matrices
    ]
    for chunk in range(4):
        columns = slice(256 * chunk, 256 * (chunk + 1))
        for rows, parts in ((slice(0, TOKENS), states), (slice(TOKENS, ROWS), notes)):
            mine[rows, columns] = jnp.where(core == 0, parts[chunk], parts[chunk + 4])
            theirs[rows, columns] = jnp.where(core == 0, parts[chunk + 4], parts[chunk])


def inside_kernel(cum, offset, docs, inputs, writes, reads, gain, out):
    scores = lax.dot_general(
        reads[...], writes[...], (((1,), (1,)), ((), ())), preferred_element_type=f32
    )
    column = document_column(docs[...])
    column = jnp.concatenate([column, column], axis=1)
    linked = (column == docs[...].astype(f32)) & (
        iota(TOKENS, TOKENS, 0) >= iota(TOKENS, TOKENS, 1)
    )
    scores = jnp.where(linked, scores, 0.0)
    upper = scores[:128, :128]
    lower = scores[128:]
    left = iota(TOKENS, 128, 1) < WIDTH
    for pair in range(HEADS // 2):
        columns = slice(128 * pair, 128 * (pair + 1))
        u = inputs[:, columns]
        zero = jnp.zeros_like(u)
        top = bottom = None
        for side in range(2):
            head = 2 * pair + side
            part = jnp.where(left, u, zero) if side == 0 else jnp.where(left, zero, u)
            ci = cum[:, head : head + 1]
            cj = offset[head : head + 1, :]
            first = (jnp.exp(ci[:128] - cj[:, :128]) * upper).astype(bf16)
            second = (jnp.exp(ci[128:] - cj) * lower).astype(bf16)
            first = jnp.dot(first, part[:128], preferred_element_type=f32)
            second = jnp.dot(second, part, preferred_element_type=f32)
            top = first if top is None else top + first
            bottom = second if bottom is None else bottom + second
        gains = jnp.where(
            left[:1], gain[:, 2 * pair : 2 * pair + 1], gain[:, 2 * pair + 1 : 2 * pair + 2]
        )
        wide = u.astype(f32) * gains
        out[:128, columns] = top + wide[:128]
        out[128:, columns] = bottom + wide[128:]


def described(ref_rows):
    rows = ref_rows.astype(f32)
    return rows[0:1] + rows[1:2] + rows[2:3], rows[3:4]


def meta_rows(total, last):
    high, middle, low = [part.astype(f32) for part in split3(total)]
    row = iota(META, total.shape[1], 0)
    return jnp.where(
        row == 0,
        high,
        jnp.where(row == 1, middle, jnp.where(row == 2, low, jnp.where(row == 3, last, 0.0))),
    ).astype(bf16)


def joined(earlier, later):
    total = earlier[1] + later[1]
    keep = jnp.where(later[2] == earlier[2], jnp.exp(later[1]), 0.0)
    return keep * earlier[0] + later[0], total, later[2]


def unpacked(payload):
    total, last = described(payload[TOKENS:])
    return payload[:TOKENS].astype(f32), total, last


def chip_kernel(mine, other, *outs):
    _, z, core = context_place()
    for step in range(4):
        columns = pl.ds(pl.multiple_of(((z + step) % 4) * QUARTER, QUARTER), QUARTER)
        own, near = mine[:, columns], other[:, columns]
        first = unpacked(jnp.where(core == 0, own, near))
        second = unpacked(jnp.where(core == 0, near, own))
        state, total, last = joined(first, second)
        outs[step][:TOKENS] = state.astype(bf16)
        outs[step][TOKENS:] = meta_rows(total, last)


def picked(slots, index):
    value = slots[0]
    for number in range(1, len(slots)):
        value = jnp.where(index == number, slots[number], value)
    return value


def row_kernel(a0, a1, a2, a3, out):
    _, z, _ = context_place()
    slots = [ref[...] for ref in (a0, a1, a2, a3)]
    whole = unpacked(picked(slots, z))
    for chip in range(1, 4):
        whole = joined(whole, unpacked(picked(slots, (z - chip) % 4)))
    out[:TOKENS] = whole[0].astype(bf16)
    out[TOKENS:] = meta_rows(whole[1], whole[2])


def entering_kernel(a0, a1, a2, a3, near, far, *outs):
    _, z, _ = context_place()
    slots = [ref[...] for ref in (a0, a1, a2, a3)]
    current = joined(unpacked(far[...]), unpacked(near[...]))
    entering = []
    for chip in range(4):
        entering.append((current[0].astype(bf16), meta_rows(current[1], current[2])))
        if chip < 3:
            current = joined(current, unpacked(picked(slots, (z - chip) % 4)))
    for step in range(4):
        outs[step][:TOKENS] = picked([e[0] for e in entering], (z + step) % 4)
        outs[step][TOKENS:] = picked([e[1] for e in entering], (z + step) % 4)


def core_kernel(b0, b1, b2, b3, mine, other, keep, send):
    _, z, core = context_place()
    for step, ref in enumerate((b0, b1, b2, b3)):
        columns = pl.ds(pl.multiple_of(((z - step) % 4) * QUARTER, QUARTER), QUARTER)
        first = ref[...]
        written = unpacked(jnp.where(core == 0, mine[:, columns], other[:, columns]))
        state, total, last = joined(unpacked(first), written)
        second = jnp.concatenate([state.astype(bf16), meta_rows(total, last)], axis=0)
        keep[:, columns] = jnp.where(core == 0, first, second)
        send[:, columns] = jnp.where(core == 0, second, first)


def carried_kernel(inside, cum, docs, reads, keep, other, out):
    _, _, core = context_place()
    before = keep[TOKENS:, :HEADS][3:4].astype(f32)
    column = document_column(docs[...])[:, :HEADS]
    factor = jnp.where(column == before, jnp.exp(cum[...]), 0.0)
    halves = [jnp.where(core == 0, keep[:TOKENS], other[:TOKENS])]
    halves.append(jnp.where(core == 0, other[:TOKENS], keep[:TOKENS]))
    carried = [
        jnp.dot(
            reads[...],
            halves[chunk // 4][:, 256 * (chunk % 4) : 256 * (chunk % 4 + 1)],
            preferred_element_type=f32,
        )
        for chunk in range(8)
    ]
    factor = two_parts(factor)
    scale = [spread(factor, spread_matrix(chunk)) for chunk in range(8)]
    for chunk in range(8):
        columns = slice(256 * chunk, 256 * (chunk + 1))
        out[:, columns] = (inside[:, columns] + carried[chunk] * scale[chunk]).astype(bf16)


def cut_kernel(keys, values, *refs):
    outs, semaphores = refs[:4], refs[4]
    x = lax.axis_index("tensor")
    sources, targets = [], []
    for step in range(4):
        columns = pl.ds(pl.multiple_of(((x + step) % 4) * DIM, DIM), DIM)
        sources += [keys.at[:, columns], values.at[:, columns]]
        targets += [outs[step].at[:, :DIM], outs[step].at[:, DIM:]]
    for copy in fetch(sources, targets, semaphores):
        copy.wait()


def assemble_kernel(p0, p1, p2, p3, docs, out):
    x = lax.axis_index("tensor")
    for step, ref in enumerate((p0, p1, p2, p3)):
        out[pl.ds(pl.multiple_of(((x - step) % 4) * 64, 64), 64), :] = ref[...]
    first = jnp.sum(jnp.where(docs[...] >= 1, 1.0, 0.0), axis=1, keepdims=True)
    second = jnp.sum(jnp.where(docs[...] >= 2, 1.0, 0.0), axis=1, keepdims=True)
    lane = iota(META, 2 * DIM, 1)
    counts = jnp.where(lane == 1, first, jnp.where(lane == 2, second, 0.0))
    out[TOKENS:] = jnp.where(lane == 0, float(TOKENS), counts).astype(bf16)


def chunk_kernel(mine, other, out):
    _, _, core = context_place()
    out[:ROWS] = jnp.where(core == 0, mine[...], other[...])
    out[ROWS:] = jnp.where(core == 0, other[...], mine[...])


def far_kernel(chunk, above, *outs):
    _, z, core = context_place()
    for step in range(1, 4):
        own = (core == 1) & ((z + step) % 4 > z)
        outs[step - 1][...] = jnp.where(own, chunk[...], above[...])


def bundle_kernel(a0, a1, a2, a3, out):
    for step, ref in enumerate((a0, a1, a2, a3)):
        out[2 * ROWS * step : 2 * ROWS * (step + 1)] = ref[...]


def chunk_of(blocks):
    one, two = blocks
    keys = jnp.concatenate([one[:, :DIM], two[:, :DIM]], axis=0)
    values = jnp.concatenate([one[:, DIM:], two[:, DIM:]], axis=0)
    values = jnp.concatenate([values.T, jnp.ones((META, CHUNK), bf16)], axis=0)
    return jnp.concatenate([keys, keys], axis=1), values


def mask_of(chunk, token, lowest):
    place = chunk * CHUNK + iota(CHUNK, TOKENS, 0)
    return jnp.where((place <= token) & (place >= lowest), 0.0, negative)


def fold(keys, values, bias, turned, peaks, sums, kind):
    def score(head):
        scores = jnp.dot(keys, turned[head], preferred_element_type=f32)
        return scores if bias is None else scores + bias

    def add(head, weights, shrink):
        new = jnp.dot(values, weights, preferred_element_type=f32)
        if kind == "first":
            sums[head] = new
        elif kind == "fixed":
            sums[head] = sums[head] + new
        else:
            sums[head] = sums[head] * shrink + new

    ahead = [score(head) for head in range(LEAD)]
    pending = None
    for head in range(REPEATS):
        if head + LEAD < REPEATS:
            ahead.append(score(head + LEAD))
        scores = ahead[head]
        shrink = None
        if kind == "fixed":
            new = peaks[head : head + 1]
        else:
            new = jnp.max(scores, axis=0, keepdims=True)
            if kind == "online":
                old = peaks[head : head + 1]
                new = jnp.maximum(old, new)
                shrink = jnp.exp2(old - new)
            peaks[head : head + 1] = new
        weights = jnp.exp2(scores - new).astype(bf16)
        if pending is not None:
            add(*pending)
        pending = (head, weights, shrink)
    add(*pending)


def starts_of(ids, start, base):
    below_one = jnp.sum(jnp.where(ids < 1, 1.0, 0.0)).astype(jnp.int32)
    below_two = jnp.sum(jnp.where(ids < 2, 1.0, 0.0)).astype(jnp.int32)
    opening = jnp.min(ids)
    return jnp.where(ids == opening, start, base + jnp.where(ids == 1, below_one, below_two))


def counted(counts, opening):
    here = (iota(META, 128, 0) == 0) & (iota(META, 128, 1) == opening)
    return jnp.sum(jnp.where(here, counts, 0.0)).astype(jnp.int32)


def own_kernel(queries, docs, chunk_ref, turned, peaks, sums):
    y, z, core = context_place()
    base = lax.axis_index("context") * TOKENS
    ids = docs[...]
    earlier = jnp.where(core == 1, chunk_ref[TOKENS:ROWS, :128].astype(f32), 0.0)
    lowest = starts_of(ids, base - counted(earlier, jnp.min(ids)), base)
    factor = math.log2(math.e) / math.sqrt(DIM)
    for head in range(REPEATS):
        scaled = (queries[:, head * DIM : (head + 1) * DIM].astype(f32) * factor).T
        high, middle, _ = split3(scaled)
        turned[head, :DIM] = high
        turned[head, DIM:] = middle
    bias = mask_of(y * 4 + z, base + iota(1, TOKENS, 1), lowest)
    keys, values = chunk_of([chunk_ref[:TOKENS], chunk_ref[ROWS : ROWS + TOKENS]])
    fold(keys, values, bias, turned, peaks, sums, "first")


def attention_kernel(docs, chunk_ref, bundle, arrived, turned, own_peaks, own_sums, out, peaks, sums):
    sums[...] = own_sums[...]
    y, z, core = context_place()
    base = lax.axis_index("context") * TOKENS
    own = y * 4 + z
    ids = docs[...]
    counts = jnp.where(core == 1, chunk_ref[TOKENS:ROWS, :128].astype(f32), 0.0)
    for block in range(8):
        rows = slice(block * ROWS + TOKENS, (block + 1) * ROWS)
        counts = counts + bundle[rows, :128].astype(f32) + arrived[rows, :128].astype(f32)
    start = base - counted(counts, jnp.min(ids))
    lowest = starts_of(ids, start, base)
    token = base + iota(1, TOKENS, 1)

    def visit(chunk, masked, peaks, kind):
        near = chunk // 4 == y - 1
        slot = ((z - chunk) % 4) * 2 * ROWS
        blocks = []
        for block in range(2):
            place = pl.ds(pl.multiple_of(slot + block * ROWS, ROWS), TOKENS)
            blocks.append(jnp.where(near == (core == 0), bundle[place, :], arrived[place, :]))
        keys, values = chunk_of(blocks)
        bias = mask_of(chunk, token, lowest) if masked else None
        fold(keys, values, bias, turned, peaks, sums, kind)

    first = start // CHUNK
    clear = jnp.minimum((jnp.max(lowest) + CHUNK - 1) // CHUNK, own)

    @pl.loop(first, clear)
    def _(chunk):
        visit(chunk, True, own_peaks, "fixed")

    @pl.loop(clear, own)
    def _(chunk):
        visit(chunk, False, own_peaks, "fixed")

    worst = jnp.max(jnp.concatenate([sums[head, DIM : DIM + 1] for head in range(REPEATS)], axis=0))

    @pl.when(jnp.logical_not(worst < 1e30))
    def _():
        peaks[...] = own_peaks[...]
        sums[...] = own_sums[...]

        @pl.loop(first, own)
        def _(chunk):
            visit(chunk, True, peaks, "online")

    for head in range(REPEATS):
        result = sums[head, :DIM] * (1.0 / sums[head, DIM : DIM + 1])
        out[:, head * DIM : (head + 1) * DIM] = result.T.astype(bf16)


def around_z(steps):
    return [
        (y * 8 + z * 2 + k, y * 8 + ((z + steps) % 4) * 2 + k)
        for y in range(4)
        for z in range(4)
        for k in range(2)
    ]


def along_y(steps):
    return [(c, c + 8 * steps) for c in range(BLOCKS - 8 * steps)]


def body(
    mixer_input,
    step_raw,
    step_bias,
    decay_log,
    skip_gain,
    write_keys,
    read_keys,
    document_ids,
    query_rows,
    key_rows,
    value_rows,
):
    docs = document_ids.reshape(1, TOKENS)
    across = [(c, c ^ 1) for c in range(BLOCKS)]
    below = [(c, c + 8 * (1 + c % 2)) for c in range(BLOCKS) if c + 8 * (1 + c % 2) < BLOCKS]

    cuts = run(
        cut_kernel,
        "cut_keys",
        [shape(64, 2 * DIM)] * 4,
        key_rows,
        value_rows,
        far=(0, 1),
        scratch=[pltpu.SemaphoreType.DMA((8,))],
        mib=56,
    )
    parts = [cuts[0]] + [
        lax.ppermute(cuts[step], "tensor", [(x, (x + step) % 4) for x in range(4)])
        for step in (1, 2, 3)
    ]

    mine, theirs, cum, offset = run(
        write_kernel,
        "mixer_write",
        [shape(ROWS, HALF), shape(ROWS, HALF), shape(TOKENS, HEADS, f32), shape(HEADS, TOKENS, f32)],
        step_raw.T,
        step_bias.reshape(1, HEADS),
        decay_log.reshape(1, HEADS),
        docs,
        mixer_input,
        write_keys,
        far=range(6),
        scratch=[
            pltpu.VMEM((HEADS, TOKENS), f32),
            pltpu.VMEM((1, HEADS), f32),
            pltpu.VMEM((1, HEADS), f32),
            pltpu.VMEM((1, TOKENS), jnp.int32),
            pltpu.VMEM((TOKENS, HEADS * WIDTH), bf16),
            pltpu.VMEM((TOKENS, DSTATE), bf16),
            pltpu.SemaphoreType.DMA((6,)),
        ],
        mib=56,
        flops=2 * 256 * 256 * 2048,
    )
    parts, mine, theirs, cum, offset = lax.optimization_barrier((parts, mine, theirs, cum, offset))
    (block,) = run(assemble_kernel, "assemble_keys", [shape(ROWS, 2 * DIM)], *parts, docs)
    other_block = lax.ppermute(block, "context", across)
    other = lax.ppermute(theirs, "context", across)

    quarter = [shape(ROWS, QUARTER)]
    (chunk,) = run(chunk_kernel, "chunk_keys", [shape(2 * ROWS, 2 * DIM)], block, other_block)
    above = lax.ppermute(chunk, "context", below)
    other, chunk = lax.optimization_barrier((other, chunk))
    chips = run(chip_kernel, "chip_state", quarter * 4, mine, other)
    slots = [chips[0]] + [lax.ppermute(chips[s], "context", around_z(s)) for s in (1, 2, 3)]

    (inside,) = run(
        inside_kernel,
        "mixer_inside",
        [shape(TOKENS, HEADS * WIDTH, f32)],
        cum,
        offset,
        docs,
        mixer_input,
        write_keys,
        read_keys,
        skip_gain.reshape(1, HEADS),
        mib=24,
        flops=2 * 256 * 256 * 128 * 32,
    )

    above, inside = lax.optimization_barrier((above, inside))
    far_cuts = run(far_kernel, "far_keys", [shape(2 * ROWS, 2 * DIM)] * 3, chunk, above)
    far = [lax.ppermute(far_cuts[s - 1], "context", around_z(s)) for s in (1, 2, 3)]

    slots, far_cuts = lax.optimization_barrier((slots, far_cuts))
    (row,) = run(row_kernel, "row_state", quarter, *slots)
    near_row = lax.ppermute(row, "context", along_y(1))
    far_row = lax.ppermute(row, "context", along_y(2))
    turned, peaks, sums = run(
        own_kernel,
        "attention_own",
        [
            jax.ShapeDtypeStruct((REPEATS, 2 * DIM, TOKENS), bf16),
            shape(REPEATS, TOKENS, f32),
            jax.ShapeDtypeStruct((REPEATS, DIM + META, TOKENS), f32),
        ],
        query_rows,
        docs,
        chunk,
        mib=24,
        flops=4 * 2048 * 512 * 128,
        transcendentals=2048 * 512,
    )
    near_row, far_row, turned = lax.optimization_barrier((near_row, far_row, turned))
    entering = run(entering_kernel, "entering_state", quarter * 4, *slots, near_row, far_row)
    back = [entering[0]] + [lax.ppermute(entering[s], "context", around_z(s)) for s in (1, 2, 3)]

    far, entering = lax.optimization_barrier((far, entering))
    (bundle,) = run(bundle_kernel, "bundle_keys", [shape(8 * ROWS, 2 * DIM)], above, *far)
    arrived = lax.ppermute(bundle, "context", across)

    (attended,) = run(
        attention_kernel,
        "attention",
        [shape(TOKENS, REPEATS * DIM)],
        docs,
        chunk,
        bundle,
        arrived,
        turned,
        peaks,
        sums,
        scratch=[
            pltpu.VMEM((REPEATS, TOKENS), f32),
            pltpu.VMEM((REPEATS, DIM + META, TOKENS), f32),
        ],
        mib=32,
        flops=4 * 2048 * 4096 * 128,
        transcendentals=2048 * 4096,
    )
    back, attended = lax.optimization_barrier((back, attended))

    keep, send = run(core_kernel, "core_state", [shape(ROWS, HALF)] * 2, *back, mine, other)
    state_arrived = lax.ppermute(send, "context", across)
    (mixed,) = run(
        carried_kernel,
        "mixer_carried",
        [shape(TOKENS, HEADS * WIDTH)],
        inside,
        cum,
        docs,
        read_keys,
        keep,
        state_arrived,
        mib=24,
        flops=2 * 256 * 256 * 2048,
    )
    return mixed, attended


def solution(mesh):
    placed = (
        P("context", "tensor"),
        P("context", "tensor"),
        P("tensor"),
        P("tensor"),
        P("tensor"),
        P("context", "tensor"),
        P("context", "tensor"),
        P("context"),
        P("context", "tensor"),
        P(("context", "tensor"), None),
        P(("context", "tensor"), None),
    )
    return jax.shard_map(
        body,
        mesh=mesh,
        in_specs=placed,
        out_specs=(P("context", "tensor"), P("context", "tensor")),
        check_vma=False,
    )
```

```python
import functools
import math

import jax
import jax.numpy as jnp
from jax import lax
from jax.experimental import pallas as pl
from jax.experimental.pallas import tpu as pltpu
from jax.sharding import PartitionSpec as P

TOKENS = 256
HEADS = 32
WIDTH = 64
DSTATE = 256
REPEATS = 8
DIM = 128
META = 16
ROWS = TOKENS + META
HALF = HEADS * WIDTH // 2
QUARTER = HALF // 4
CHUNK = 2 * TOKENS
BLOCKS = 32
LEAD = 3

f32 = jnp.float32
bf16 = jnp.bfloat16
highest = lax.Precision.HIGHEST
negative = -1e30


def context_place():
    position = lax.axis_index("context")
    return position // 8, (position // 2) % 4, position % 2


def run(
    kernel, name, outs, *args, far=(), onto=None, scratch=(), mib=16, flops=0, transcendentals=0
):
    moved = sum(math.prod(a.shape) * a.dtype.itemsize for a in args)
    moved += sum(math.prod(a.shape) * a.dtype.itemsize for a in outs)
    spaces = [pltpu.HBM if number in far else pltpu.VMEM for number in range(len(args))]
    return pl.pallas_call(
        kernel,
        out_shape=outs,
        in_specs=[pl.BlockSpec(memory_space=space) for space in spaces],
        out_specs=[pl.BlockSpec(memory_space=pltpu.VMEM if onto is None else pltpu.HBM)] * len(outs),
        input_output_aliases={onto: 0} if onto is not None and onto >= 0 else {},
        scratch_shapes=list(scratch),
        compiler_params=pltpu.CompilerParams(vmem_limit_bytes=mib << 20),
        cost_estimate=pl.CostEstimate(
            flops=flops, bytes_accessed=moved, transcendentals=transcendentals
        ),
        name=name,
    )(*args)


def shape(rows, columns, dtype=bf16):
    return jax.ShapeDtypeStruct((rows, columns), dtype)


def iota(rows, columns, axis):
    return lax.broadcasted_iota(jnp.int32, (rows, columns), axis)


def split3(value):
    high = value.astype(bf16)
    rest = value - high.astype(f32)
    middle = rest.astype(bf16)
    low = (rest - middle.astype(f32)).astype(bf16)
    return high, middle, low


def spread_matrix(chunk, offset=0):
    column = iota(2 * HEADS, 256, 1) + 256 * chunk + offset
    return (column // WIDTH == iota(2 * HEADS, 256, 0) % HEADS).astype(bf16)


def two_parts(value):
    high, middle, _ = split3(value)
    return jnp.concatenate([high, middle], axis=1)


def spread(parts, matrix):
    return jnp.dot(parts, matrix, preferred_element_type=f32)


def document_column(docs_row):
    return jnp.broadcast_to(docs_row.astype(f32), (128, TOKENS)).T


def fetch(sources, targets, semaphores):
    copies = [
        pltpu.make_async_copy(source, target, semaphores.at[number])
        for number, (source, target) in enumerate(zip(sources, targets))
    ]
    for copy in copies:
        copy.start()
    return copies


def write_kernel(*refs):
    far, (mine, theirs, cum_out, offset_out), held, semaphores = refs[:6], refs[6:10], refs[10:16], refs[16]
    copies = fetch(far, held, semaphores)
    raw, bias, decay, docs, inputs, writes = held
    _, _, core = context_place()
    for copy in copies[:4]:
        copy.wait()
    padded = jnp.concatenate([raw[...], jnp.zeros((128 - HEADS, TOKENS), f32)], axis=0)
    u = padded.T[:, :HEADS] + bias[...]
    step = jnp.maximum(u, 0.0) + jnp.log1p(jnp.exp(-jnp.abs(u)))
    logdec = -step * jnp.exp(decay[...])
    triangle = (iota(TOKENS, TOKENS, 0) >= iota(TOKENS, TOKENS, 1)).astype(f32)
    cum = jnp.dot(triangle, logdec, precision=highest, preferred_element_type=f32)
    cum_out[...] = cum
    offset = cum - jnp.log(step)
    padded = jnp.concatenate([offset, jnp.zeros((TOKENS, 128 - HEADS), f32)], axis=1)
    offset_out[...] = padded.T[:HEADS]
    total = cum[TOKENS - 1 :]
    column = document_column(docs[...])[:, :HEADS]
    last = column[TOKENS - 1 :]
    trail = jnp.where(column == last, jnp.exp(total - cum), 0.0) * step
    high, middle, low = [part.astype(f32) for part in split3(total)]
    row = iota(META, HEADS, 0)
    meta = jnp.where(
        row == 0,
        high,
        jnp.where(row == 1, middle, jnp.where(row == 2, low, jnp.where(row == 3, last, 0.0))),
    ).astype(bf16)
    copies[5].wait()
    turned = writes[...].T
    copies[4].wait()
    matrices = [spread_matrix(chunk) for chunk in range(8)]
    trail = two_parts(trail)
    wide = [spread(trail, matrix) for matrix in matrices]
    scaled = [
        (inputs[:, 256 * chunk : 256 * (chunk + 1)].astype(f32) * wide[chunk]).astype(bf16)
        for chunk in range(8)
    ]
    states = [
        jnp.dot(turned, part, preferred_element_type=f32).astype(bf16) for part in scaled
    ]
    notes = [
        jnp.dot(meta, matrix[:HEADS], preferred_element_type=f32).astype(bf16) for matrix in matrices
    ]
    for chunk in range(4):
        columns = slice(256 * chunk, 256 * (chunk + 1))
        for rows, parts in ((slice(0, TOKENS), states), (slice(TOKENS, ROWS), notes)):
            mine[rows, columns] = jnp.where(core == 0, parts[chunk], parts[chunk + 4])
            theirs[rows, columns] = jnp.where(core == 0, parts[chunk + 4], parts[chunk])


def inside_kernel(cum, offset, docs, inputs, writes, reads, gain, out):
    scores = lax.dot_general(
        reads[...], writes[...], (((1,), (1,)), ((), ())), preferred_element_type=f32
    )
    column = document_column(docs[...])
    column = jnp.concatenate([column, column], axis=1)
    linked = (column == docs[...].astype(f32)) & (
        iota(TOKENS, TOKENS, 0) >= iota(TOKENS, TOKENS, 1)
    )
    scores = jnp.where(linked, scores, 0.0)
    upper = scores[:128, :128]
    lower = scores[128:]
    left = iota(TOKENS, 128, 1) < WIDTH
    for pair in range(HEADS // 2):
        columns = slice(128 * pair, 128 * (pair + 1))
        u = inputs[:, columns]
        zero = jnp.zeros_like(u)
        top = bottom = None
        for side in range(2):
            head = 2 * pair + side
            part = jnp.where(left, u, zero) if side == 0 else jnp.where(left, zero, u)
            ci = cum[:, head : head + 1]
            cj = offset[head : head + 1, :]
            first = (jnp.exp(ci[:128] - cj[:, :128]) * upper).astype(bf16)
            second = (jnp.exp(ci[128:] - cj) * lower).astype(bf16)
            first = jnp.dot(first, part[:128], preferred_element_type=f32)
            second = jnp.dot(second, part, preferred_element_type=f32)
            top = first if top is None else top + first
            bottom = second if bottom is None else bottom + second
        gains = jnp.where(
            left[:1], gain[:, 2 * pair : 2 * pair + 1], gain[:, 2 * pair + 1 : 2 * pair + 2]
        )
        wide = u.astype(f32) * gains
        out[:128, columns] = top + wide[:128]
        out[128:, columns] = bottom + wide[128:]


def described(ref_rows):
    rows = ref_rows.astype(f32)
    return rows[0:1] + rows[1:2] + rows[2:3], rows[3:4]


def meta_rows(total, last):
    high, middle, low = [part.astype(f32) for part in split3(total)]
    row = iota(META, total.shape[1], 0)
    return jnp.where(
        row == 0,
        high,
        jnp.where(row == 1, middle, jnp.where(row == 2, low, jnp.where(row == 3, last, 0.0))),
    ).astype(bf16)


def joined(earlier, later):
    total = earlier[1] + later[1]
    keep = jnp.where(later[2] == earlier[2], jnp.exp(later[1]), 0.0)
    return keep * earlier[0] + later[0], total, later[2]


def unpacked(payload):
    total, last = described(payload[TOKENS:])
    return payload[:TOKENS].astype(f32), total, last


def chip_kernel(mine, other, *outs):
    _, z, core = context_place()
    for step in range(4):
        columns = pl.ds(pl.multiple_of(((z + step) % 4) * QUARTER, QUARTER), QUARTER)
        own, near = mine[:, columns], other[:, columns]
        first = unpacked(jnp.where(core == 0, own, near))
        second = unpacked(jnp.where(core == 0, near, own))
        state, total, last = joined(first, second)
        outs[step][:TOKENS] = state.astype(bf16)
        outs[step][TOKENS:] = meta_rows(total, last)


def picked(slots, index):
    value = slots[0]
    for number in range(1, len(slots)):
        value = jnp.where(index == number, slots[number], value)
    return value


def row_kernel(a0, a1, a2, a3, out):
    _, z, _ = context_place()
    slots = [ref[...] for ref in (a0, a1, a2, a3)]
    whole = unpacked(picked(slots, z))
    for chip in range(1, 4):
        whole = joined(whole, unpacked(picked(slots, (z - chip) % 4)))
    out[:TOKENS] = whole[0].astype(bf16)
    out[TOKENS:] = meta_rows(whole[1], whole[2])


def entering_kernel(a0, a1, a2, a3, near, far, *outs):
    _, z, _ = context_place()
    slots = [ref[...] for ref in (a0, a1, a2, a3)]
    current = joined(unpacked(far[...]), unpacked(near[...]))
    entering = []
    for chip in range(4):
        entering.append((current[0].astype(bf16), meta_rows(current[1], current[2])))
        if chip < 3:
            current = joined(current, unpacked(picked(slots, (z - chip) % 4)))
    for step in range(4):
        outs[step][:TOKENS] = picked([e[0] for e in entering], (z + step) % 4)
        outs[step][TOKENS:] = picked([e[1] for e in entering], (z + step) % 4)


def core_kernel(b0, b1, b2, b3, mine, other, keep, send):
    _, z, core = context_place()
    for step, ref in enumerate((b0, b1, b2, b3)):
        columns = pl.ds(pl.multiple_of(((z - step) % 4) * QUARTER, QUARTER), QUARTER)
        first = ref[...]
        written = unpacked(jnp.where(core == 0, mine[:, columns], other[:, columns]))
        state, total, last = joined(unpacked(first), written)
        second = jnp.concatenate([state.astype(bf16), meta_rows(total, last)], axis=0)
        keep[:, columns] = jnp.where(core == 0, first, second)
        send[:, columns] = jnp.where(core == 0, second, first)


def carried_kernel(part, inside, cum, docs, reads, keep, state, *refs):
    out, held, semaphores = refs[part:]
    _, _, core = context_place()
    before = keep[TOKENS:, :HEADS][3:4].astype(f32)
    column = document_column(docs[...])[:, :HEADS]
    factor = two_parts(jnp.where(column == before, jnp.exp(cum[...]), 0.0))
    half = core if part == 0 else 1 - core
    offset = pl.multiple_of(half * HALF, HALF)
    carried = [
        jnp.dot(
            reads[...],
            state[:TOKENS, 256 * chunk : 256 * (chunk + 1)],
            preferred_element_type=f32,
        )
        for chunk in range(4)
    ]
    scale = [spread(factor, spread_matrix(chunk, offset)) for chunk in range(4)]
    copies = []
    for chunk in range(4):
        columns = pl.ds(pl.multiple_of(offset + 256 * chunk, 256), 256)
        local = slice(256 * chunk, 256 * (chunk + 1))
        result = inside[:, columns] + carried[chunk] * scale[chunk]
        held[:, local] = result.astype(bf16)
        copies += fetch([held.at[:, local]], [out.at[:, columns]], semaphores.at[pl.ds(chunk, 1)])
    for copy in copies:
        copy.wait()


def cut_kernel(keys, values, *refs):
    outs, semaphores = refs[:4], refs[4]
    x = lax.axis_index("tensor")
    sources, targets = [], []
    for step in range(4):
        columns = pl.ds(pl.multiple_of(((x + step) % 4) * DIM, DIM), DIM)
        sources += [keys.at[:, columns], values.at[:, columns]]
        targets += [outs[step].at[:, :DIM], outs[step].at[:, DIM:]]
    for copy in fetch(sources, targets, semaphores):
        copy.wait()


def assemble_kernel(p0, p1, p2, p3, docs, out):
    x = lax.axis_index("tensor")
    for step, ref in enumerate((p0, p1, p2, p3)):
        out[pl.ds(pl.multiple_of(((x - step) % 4) * 64, 64), 64), :] = ref[...]
    first = jnp.sum(jnp.where(docs[...] >= 1, 1.0, 0.0), axis=1, keepdims=True)
    second = jnp.sum(jnp.where(docs[...] >= 2, 1.0, 0.0), axis=1, keepdims=True)
    lane = iota(META, 2 * DIM, 1)
    counts = jnp.where(lane == 1, first, jnp.where(lane == 2, second, 0.0))
    out[TOKENS:] = jnp.where(lane == 0, float(TOKENS), counts).astype(bf16)


def chunk_kernel(mine, other, out):
    _, _, core = context_place()
    out[:ROWS] = jnp.where(core == 0, mine[...], other[...])
    out[ROWS:] = jnp.where(core == 0, other[...], mine[...])


def far_kernel(chunk, above, *outs):
    _, z, core = context_place()
    for step in range(1, 4):
        own = (core == 1) & ((z + step) % 4 > z)
        outs[step - 1][...] = jnp.where(own, chunk[...], above[...])


def bundle_kernel(a0, a1, a2, a3, out):
    for step, ref in enumerate((a0, a1, a2, a3)):
        out[2 * ROWS * step : 2 * ROWS * (step + 1)] = ref[...]


def chunk_of(blocks):
    one, two = blocks
    keys = jnp.concatenate([one[:, :DIM], two[:, :DIM]], axis=0)
    values = jnp.concatenate([one[:, DIM:], two[:, DIM:]], axis=0)
    values = jnp.concatenate([values.T, jnp.ones((META, CHUNK), bf16)], axis=0)
    return jnp.concatenate([keys, keys], axis=1), values


def mask_of(chunk, token, lowest):
    place = chunk * CHUNK + iota(CHUNK, TOKENS, 0)
    return jnp.where((place <= token) & (place >= lowest), 0.0, negative)


def fold(keys, values, bias, turned, peaks, sums, kind):
    def score(head):
        scores = jnp.dot(keys, turned[head], preferred_element_type=f32)
        return scores if bias is None else scores + bias

    def add(head, weights, shrink):
        new = jnp.dot(values, weights, preferred_element_type=f32)
        if kind == "first":
            sums[head] = new
        elif kind == "fixed":
            sums[head] = sums[head] + new
        else:
            sums[head] = sums[head] * shrink + new

    ahead = [score(head) for head in range(LEAD)]
    pending = None
    for head in range(REPEATS):
        if head + LEAD < REPEATS:
            ahead.append(score(head + LEAD))
        scores = ahead[head]
        shrink = None
        if kind == "fixed":
            new = peaks[head : head + 1]
        else:
            new = jnp.max(scores, axis=0, keepdims=True)
            if kind == "online":
                old = peaks[head : head + 1]
                new = jnp.maximum(old, new)
                shrink = jnp.exp2(old - new)
            peaks[head : head + 1] = new
        weights = jnp.exp2(scores - new).astype(bf16)
        if pending is not None:
            add(*pending)
        pending = (head, weights, shrink)
    add(*pending)


def starts_of(ids, start, base):
    below_one = jnp.sum(jnp.where(ids < 1, 1.0, 0.0)).astype(jnp.int32)
    below_two = jnp.sum(jnp.where(ids < 2, 1.0, 0.0)).astype(jnp.int32)
    opening = jnp.min(ids)
    return jnp.where(ids == opening, start, base + jnp.where(ids == 1, below_one, below_two))


def counted(counts, opening):
    here = (iota(META, 128, 0) == 0) & (iota(META, 128, 1) == opening)
    return jnp.sum(jnp.where(here, counts, 0.0)).astype(jnp.int32)


def own_kernel(queries, docs, chunk_ref, turned, peaks, sums):
    y, z, core = context_place()
    base = lax.axis_index("context") * TOKENS
    ids = docs[...]
    earlier = jnp.where(core == 1, chunk_ref[TOKENS:ROWS, :128].astype(f32), 0.0)
    lowest = starts_of(ids, base - counted(earlier, jnp.min(ids)), base)
    factor = math.log2(math.e) / math.sqrt(DIM)
    for head in range(REPEATS):
        scaled = (queries[:, head * DIM : (head + 1) * DIM].astype(f32) * factor).T
        high, middle, _ = split3(scaled)
        turned[head, :DIM] = high
        turned[head, DIM:] = middle
    bias = mask_of(y * 4 + z, base + iota(1, TOKENS, 1), lowest)
    keys, values = chunk_of([chunk_ref[:TOKENS], chunk_ref[ROWS : ROWS + TOKENS]])
    fold(keys, values, bias, turned, peaks, sums, "first")


def attention_kernel(docs, chunk_ref, bundle, arrived, turned, own_peaks, own_sums, out, peaks, sums):
    sums[...] = own_sums[...]
    y, z, core = context_place()
    base = lax.axis_index("context") * TOKENS
    own = y * 4 + z
    ids = docs[...]
    counts = jnp.where(core == 1, chunk_ref[TOKENS:ROWS, :128].astype(f32), 0.0)
    for block in range(8):
        rows = slice(block * ROWS + TOKENS, (block + 1) * ROWS)
        counts = counts + bundle[rows, :128].astype(f32) + arrived[rows, :128].astype(f32)
    start = base - counted(counts, jnp.min(ids))
    lowest = starts_of(ids, start, base)
    token = base + iota(1, TOKENS, 1)

    def visit(chunk, masked, peaks, kind):
        near = chunk // 4 == y - 1
        slot = ((z - chunk) % 4) * 2 * ROWS
        blocks = []
        for block in range(2):
            place = pl.ds(pl.multiple_of(slot + block * ROWS, ROWS), TOKENS)
            blocks.append(jnp.where(near == (core == 0), bundle[place, :], arrived[place, :]))
        keys, values = chunk_of(blocks)
        bias = mask_of(chunk, token, lowest) if masked else None
        fold(keys, values, bias, turned, peaks, sums, kind)

    first = start // CHUNK
    clear = jnp.minimum((jnp.max(lowest) + CHUNK - 1) // CHUNK, own)

    @pl.loop(first, clear)
    def _(chunk):
        visit(chunk, True, own_peaks, "fixed")

    @pl.loop(clear, own)
    def _(chunk):
        visit(chunk, False, own_peaks, "fixed")

    worst = jnp.max(jnp.concatenate([sums[head, DIM : DIM + 1] for head in range(REPEATS)], axis=0))

    @pl.when(jnp.logical_not(worst < 1e30))
    def _():
        peaks[...] = own_peaks[...]
        sums[...] = own_sums[...]

        @pl.loop(first, own)
        def _(chunk):
            visit(chunk, True, peaks, "online")

    for head in range(REPEATS):
        result = sums[head, :DIM] * (1.0 / sums[head, DIM : DIM + 1])
        out[:, head * DIM : (head + 1) * DIM] = result.T.astype(bf16)


def around_z(steps):
    return [
        (y * 8 + z * 2 + k, y * 8 + ((z + steps) % 4) * 2 + k)
        for y in range(4)
        for z in range(4)
        for k in range(2)
    ]


def along_y(steps):
    return [(c, c + 8 * steps) for c in range(BLOCKS - 8 * steps)]


def body(
    mixer_input,
    step_raw,
    step_bias,
    decay_log,
    skip_gain,
    write_keys,
    read_keys,
    document_ids,
    query_rows,
    key_rows,
    value_rows,
):
    docs = document_ids.reshape(1, TOKENS)
    across = [(c, c ^ 1) for c in range(BLOCKS)]
    below = [(c, c + 8 * (1 + c % 2)) for c in range(BLOCKS) if c + 8 * (1 + c % 2) < BLOCKS]

    cuts = run(
        cut_kernel,
        "cut_keys",
        [shape(64, 2 * DIM)] * 4,
        key_rows,
        value_rows,
        far=(0, 1),
        scratch=[pltpu.SemaphoreType.DMA((8,))],
        mib=56,
    )
    parts = [cuts[0]] + [
        lax.ppermute(cuts[step], "tensor", [(x, (x + step) % 4) for x in range(4)])
        for step in (1, 2, 3)
    ]

    mine, theirs, cum, offset = run(
        write_kernel,
        "mixer_write",
        [shape(ROWS, HALF), shape(ROWS, HALF), shape(TOKENS, HEADS, f32), shape(HEADS, TOKENS, f32)],
        step_raw.T,
        step_bias.reshape(1, HEADS),
        decay_log.reshape(1, HEADS),
        docs,
        mixer_input,
        write_keys,
        far=range(6),
        scratch=[
            pltpu.VMEM((HEADS, TOKENS), f32),
            pltpu.VMEM((1, HEADS), f32),
            pltpu.VMEM((1, HEADS), f32),
            pltpu.VMEM((1, TOKENS), jnp.int32),
            pltpu.VMEM((TOKENS, HEADS * WIDTH), bf16),
            pltpu.VMEM((TOKENS, DSTATE), bf16),
            pltpu.SemaphoreType.DMA((6,)),
        ],
        mib=56,
        flops=2 * 256 * 256 * 2048,
    )
    parts, mine, theirs, cum, offset = lax.optimization_barrier((parts, mine, theirs, cum, offset))
    (block,) = run(assemble_kernel, "assemble_keys", [shape(ROWS, 2 * DIM)], *parts, docs)
    other_block = lax.ppermute(block, "context", across)
    other = lax.ppermute(theirs, "context", across)

    quarter = [shape(ROWS, QUARTER)]
    (chunk,) = run(chunk_kernel, "chunk_keys", [shape(2 * ROWS, 2 * DIM)], block, other_block)
    above = lax.ppermute(chunk, "context", below)
    other, chunk = lax.optimization_barrier((other, chunk))
    chips = run(chip_kernel, "chip_state", quarter * 4, mine, other)
    slots = [chips[0]] + [lax.ppermute(chips[s], "context", around_z(s)) for s in (1, 2, 3)]

    (inside,) = run(
        inside_kernel,
        "mixer_inside",
        [shape(TOKENS, HEADS * WIDTH, f32)],
        cum,
        offset,
        docs,
        mixer_input,
        write_keys,
        read_keys,
        skip_gain.reshape(1, HEADS),
        mib=24,
        flops=2 * 256 * 256 * 128 * 32,
    )

    above, inside = lax.optimization_barrier((above, inside))
    far_cuts = run(far_kernel, "far_keys", [shape(2 * ROWS, 2 * DIM)] * 3, chunk, above)
    far = [lax.ppermute(far_cuts[s - 1], "context", around_z(s)) for s in (1, 2, 3)]

    slots, far_cuts = lax.optimization_barrier((slots, far_cuts))
    (row,) = run(row_kernel, "row_state", quarter, *slots)
    near_row = lax.ppermute(row, "context", along_y(1))
    far_row = lax.ppermute(row, "context", along_y(2))
    turned, peaks, sums = run(
        own_kernel,
        "attention_own",
        [
            jax.ShapeDtypeStruct((REPEATS, 2 * DIM, TOKENS), bf16),
            shape(REPEATS, TOKENS, f32),
            jax.ShapeDtypeStruct((REPEATS, DIM + META, TOKENS), f32),
        ],
        query_rows,
        docs,
        chunk,
        mib=24,
        flops=4 * 2048 * 512 * 128,
        transcendentals=2048 * 512,
    )
    near_row, far_row, turned = lax.optimization_barrier((near_row, far_row, turned))
    entering = run(entering_kernel, "entering_state", quarter * 4, *slots, near_row, far_row)
    back = [entering[0]] + [lax.ppermute(entering[s], "context", around_z(s)) for s in (1, 2, 3)]

    far, entering = lax.optimization_barrier((far, entering))
    (bundle,) = run(bundle_kernel, "bundle_keys", [shape(8 * ROWS, 2 * DIM)], above, *far)
    arrived = lax.ppermute(bundle, "context", across)

    (attended,) = run(
        attention_kernel,
        "attention",
        [shape(TOKENS, REPEATS * DIM)],
        docs,
        chunk,
        bundle,
        arrived,
        turned,
        peaks,
        sums,
        scratch=[
            pltpu.VMEM((REPEATS, TOKENS), f32),
            pltpu.VMEM((REPEATS, DIM + META, TOKENS), f32),
        ],
        mib=32,
        flops=4 * 2048 * 4096 * 128,
        transcendentals=2048 * 4096,
    )
    back, attended = lax.optimization_barrier((back, attended))

    keep, send = run(core_kernel, "core_state", [shape(ROWS, HALF)] * 2, *back, mine, other)
    state_arrived = lax.ppermute(send, "context", across)
    (own_half,) = run(
        functools.partial(carried_kernel, 0),
        "mixer_carried_own",
        [shape(TOKENS, HEADS * WIDTH)],
        inside,
        cum,
        docs,
        read_keys,
        keep,
        keep,
        onto=-1,
        scratch=[pltpu.VMEM((TOKENS, HALF), bf16), pltpu.SemaphoreType.DMA((4,))],
        mib=24,
        flops=2 * 256 * 256 * 1024,
    )
    state_arrived, own_half = lax.optimization_barrier((state_arrived, own_half))
    (mixed,) = run(
        functools.partial(carried_kernel, 1),
        "mixer_carried",
        [shape(TOKENS, HEADS * WIDTH)],
        inside,
        cum,
        docs,
        read_keys,
        keep,
        state_arrived,
        own_half,
        far=(6,),
        onto=6,
        scratch=[pltpu.VMEM((TOKENS, HALF), bf16), pltpu.SemaphoreType.DMA((4,))],
        mib=24,
        flops=2 * 256 * 256 * 1024,
    )
    return mixed, attended


def solution(mesh):
    placed = (
        P("context", "tensor"),
        P("context", "tensor"),
        P("tensor"),
        P("tensor"),
        P("tensor"),
        P("context", "tensor"),
        P("context", "tensor"),
        P("context"),
        P("context", "tensor"),
        P(("context", "tensor"), None),
        P(("context", "tensor"), None),
    )
    return jax.shard_map(
        body,
        mesh=mesh,
        in_specs=placed,
        out_specs=(P("context", "tensor"), P("context", "tensor")),
        check_vma=False,
    )
```

```python
import functools
import math

import jax
import jax.numpy as jnp
from jax import lax
from jax.experimental import pallas as pl
from jax.experimental.pallas import tpu as pltpu
from jax.sharding import PartitionSpec as P

TOKENS = 256
HEADS = 32
WIDTH = 64
DSTATE = 256
REPEATS = 8
DIM = 128
META = 16
ROWS = TOKENS + META
HALF = HEADS * WIDTH // 2
QUARTER = HALF // 4
CHUNK = 2 * TOKENS
BLOCKS = 32
LEAD = 3

f32 = jnp.float32
bf16 = jnp.bfloat16
highest = lax.Precision.HIGHEST
negative = -1e30


def context_place():
    position = lax.axis_index("context")
    return position // 8, (position // 2) % 4, position % 2


def run(
    kernel, name, outs, *args, far=(), onto=None, scratch=(), mib=16, flops=0, transcendentals=0
):
    moved = sum(math.prod(a.shape) * a.dtype.itemsize for a in args)
    moved += sum(math.prod(a.shape) * a.dtype.itemsize for a in outs)
    spaces = [pltpu.HBM if number in far else pltpu.VMEM for number in range(len(args))]
    return pl.pallas_call(
        kernel,
        out_shape=outs,
        in_specs=[pl.BlockSpec(memory_space=space) for space in spaces],
        out_specs=[pl.BlockSpec(memory_space=pltpu.VMEM if onto is None else pltpu.HBM)] * len(outs),
        input_output_aliases={onto: 0} if onto is not None and onto >= 0 else {},
        scratch_shapes=list(scratch),
        compiler_params=pltpu.CompilerParams(vmem_limit_bytes=mib << 20),
        cost_estimate=pl.CostEstimate(
            flops=flops, bytes_accessed=moved, transcendentals=transcendentals
        ),
        name=name,
    )(*args)


def shape(rows, columns, dtype=bf16):
    return jax.ShapeDtypeStruct((rows, columns), dtype)


def iota(rows, columns, axis):
    return lax.broadcasted_iota(jnp.int32, (rows, columns), axis)


def split3(value):
    high = value.astype(bf16)
    rest = value - high.astype(f32)
    middle = rest.astype(bf16)
    low = (rest - middle.astype(f32)).astype(bf16)
    return high, middle, low


def spread_matrix(chunk, offset=0):
    column = iota(2 * HEADS, 256, 1) + 256 * chunk + offset
    return (column // WIDTH == iota(2 * HEADS, 256, 0) % HEADS).astype(bf16)


def two_parts(value):
    high, middle, _ = split3(value)
    return jnp.concatenate([high, middle], axis=1)


def spread(parts, matrix):
    return jnp.dot(parts, matrix, preferred_element_type=f32)


def document_column(docs_row):
    return jnp.broadcast_to(docs_row.astype(f32), (128, TOKENS)).T


def fetch(sources, targets, semaphores):
    copies = [
        pltpu.make_async_copy(source, target, semaphores.at[number])
        for number, (source, target) in enumerate(zip(sources, targets))
    ]
    for copy in copies:
        copy.start()
    return copies


def write_kernel(*refs):
    far, (mine, theirs, cum_out, offset_out), held, semaphores = refs[:6], refs[6:10], refs[10:16], refs[16]
    copies = fetch(far, held, semaphores)
    raw, bias, decay, docs, inputs, writes = held
    _, _, core = context_place()
    for copy in copies[:4]:
        copy.wait()
    padded = jnp.concatenate([raw[...], jnp.zeros((128 - HEADS, TOKENS), f32)], axis=0)
    u = padded.T[:, :HEADS] + bias[...]
    step = jnp.maximum(u, 0.0) + jnp.log1p(jnp.exp(-jnp.abs(u)))
    logdec = -step * jnp.exp(decay[...])
    triangle = (iota(TOKENS, TOKENS, 0) >= iota(TOKENS, TOKENS, 1)).astype(f32)
    cum = jnp.dot(triangle, logdec, precision=highest, preferred_element_type=f32)
    cum_out[...] = cum
    offset = cum - jnp.log(step)
    padded = jnp.concatenate([offset, jnp.zeros((TOKENS, 128 - HEADS), f32)], axis=1)
    offset_out[...] = padded.T[:HEADS]
    total = cum[TOKENS - 1 :]
    column = document_column(docs[...])[:, :HEADS]
    last = column[TOKENS - 1 :]
    trail = jnp.where(column == last, jnp.exp(total - cum), 0.0) * step
    high, middle, low = [part.astype(f32) for part in split3(total)]
    row = iota(META, HEADS, 0)
    meta = jnp.where(
        row == 0,
        high,
        jnp.where(row == 1, middle, jnp.where(row == 2, low, jnp.where(row == 3, last, 0.0))),
    ).astype(bf16)
    copies[5].wait()
    turned = writes[...].T
    copies[4].wait()
    matrices = [spread_matrix(chunk) for chunk in range(8)]
    trail = two_parts(trail)
    wide = [spread(trail, matrix) for matrix in matrices]
    scaled = [
        (inputs[:, 256 * chunk : 256 * (chunk + 1)].astype(f32) * wide[chunk]).astype(bf16)
        for chunk in range(8)
    ]
    states = [
        jnp.dot(turned, part, preferred_element_type=f32).astype(bf16) for part in scaled
    ]
    notes = [
        jnp.dot(meta, matrix[:HEADS], preferred_element_type=f32).astype(bf16) for matrix in matrices
    ]
    for chunk in range(4):
        columns = slice(256 * chunk, 256 * (chunk + 1))
        for rows, parts in ((slice(0, TOKENS), states), (slice(TOKENS, ROWS), notes)):
            mine[rows, columns] = jnp.where(core == 0, parts[chunk], parts[chunk + 4])
            theirs[rows, columns] = jnp.where(core == 0, parts[chunk + 4], parts[chunk])


def inside_kernel(cum, offset, docs, inputs, writes, reads, gain, out):
    scores = lax.dot_general(
        reads[...], writes[...], (((1,), (1,)), ((), ())), preferred_element_type=f32
    )
    column = document_column(docs[...])
    column = jnp.concatenate([column, column], axis=1)
    linked = (column == docs[...].astype(f32)) & (
        iota(TOKENS, TOKENS, 0) >= iota(TOKENS, TOKENS, 1)
    )
    scores = jnp.where(linked, scores, 0.0)
    upper = scores[:128, :128]
    lower = scores[128:]
    left = iota(TOKENS, 128, 1) < WIDTH
    for pair in range(HEADS // 2):
        columns = slice(128 * pair, 128 * (pair + 1))
        u = inputs[:, columns]
        zero = jnp.zeros_like(u)
        top = bottom = None
        for side in range(2):
            head = 2 * pair + side
            part = jnp.where(left, u, zero) if side == 0 else jnp.where(left, zero, u)
            ci = cum[:, head : head + 1]
            cj = offset[head : head + 1, :]
            first = (jnp.exp(ci[:128] - cj[:, :128]) * upper).astype(bf16)
            second = (jnp.exp(ci[128:] - cj) * lower).astype(bf16)
            first = jnp.dot(first, part[:128], preferred_element_type=f32)
            second = jnp.dot(second, part, preferred_element_type=f32)
            top = first if top is None else top + first
            bottom = second if bottom is None else bottom + second
        gains = jnp.where(
            left[:1], gain[:, 2 * pair : 2 * pair + 1], gain[:, 2 * pair + 1 : 2 * pair + 2]
        )
        wide = u.astype(f32) * gains
        out[:128, columns] = top + wide[:128]
        out[128:, columns] = bottom + wide[128:]


def described(ref_rows):
    rows = ref_rows.astype(f32)
    return rows[0:1] + rows[1:2] + rows[2:3], rows[3:4]


def meta_rows(total, last):
    high, middle, low = [part.astype(f32) for part in split3(total)]
    row = iota(META, total.shape[1], 0)
    return jnp.where(
        row == 0,
        high,
        jnp.where(row == 1, middle, jnp.where(row == 2, low, jnp.where(row == 3, last, 0.0))),
    ).astype(bf16)


def joined(earlier, later):
    total = earlier[1] + later[1]
    keep = jnp.where(later[2] == earlier[2], jnp.exp(later[1]), 0.0)
    return keep * earlier[0] + later[0], total, later[2]


def unpacked(payload):
    total, last = described(payload[TOKENS:])
    return payload[:TOKENS].astype(f32), total, last


def chip_kernel(mine, other, *outs):
    _, z, core = context_place()
    for step in range(4):
        columns = pl.ds(pl.multiple_of(((z + step) % 4) * QUARTER, QUARTER), QUARTER)
        own, near = mine[:, columns], other[:, columns]
        first = unpacked(jnp.where(core == 0, own, near))
        second = unpacked(jnp.where(core == 0, near, own))
        state, total, last = joined(first, second)
        outs[step][:TOKENS] = state.astype(bf16)
        outs[step][TOKENS:] = meta_rows(total, last)


def picked(slots, index):
    value = slots[0]
    for number in range(1, len(slots)):
        value = jnp.where(index == number, slots[number], value)
    return value


def row_kernel(a0, a1, a2, a3, out):
    _, z, _ = context_place()
    slots = [ref[...] for ref in (a0, a1, a2, a3)]
    whole = unpacked(picked(slots, z))
    for chip in range(1, 4):
        whole = joined(whole, unpacked(picked(slots, (z - chip) % 4)))
    out[:TOKENS] = whole[0].astype(bf16)
    out[TOKENS:] = meta_rows(whole[1], whole[2])


def entering_kernel(a0, a1, a2, a3, near, far, *outs):
    _, z, _ = context_place()
    slots = [ref[...] for ref in (a0, a1, a2, a3)]
    current = joined(unpacked(far[...]), unpacked(near[...]))
    entering = []
    for chip in range(4):
        entering.append((current[0].astype(bf16), meta_rows(current[1], current[2])))
        if chip < 3:
            current = joined(current, unpacked(picked(slots, (z - chip) % 4)))
    for step in range(4):
        outs[step][:TOKENS] = picked([e[0] for e in entering], (z + step) % 4)
        outs[step][TOKENS:] = picked([e[1] for e in entering], (z + step) % 4)


def core_kernel(b0, b1, b2, b3, mine, other, keep, send):
    _, z, core = context_place()
    for step, ref in enumerate((b0, b1, b2, b3)):
        columns = pl.ds(pl.multiple_of(((z - step) % 4) * QUARTER, QUARTER), QUARTER)
        first = ref[...]
        written = unpacked(jnp.where(core == 0, mine[:, columns], other[:, columns]))
        state, total, last = joined(unpacked(first), written)
        second = jnp.concatenate([state.astype(bf16), meta_rows(total, last)], axis=0)
        keep[:, columns] = jnp.where(core == 0, first, second)
        send[:, columns] = jnp.where(core == 0, second, first)


def carried_kernel(part, inside, cum, docs, reads, keep, state, *refs):
    out, held, semaphores = refs[part:]
    _, _, core = context_place()
    before = keep[TOKENS:, :HEADS][3:4].astype(f32)
    column = document_column(docs[...])[:, :HEADS]
    factor = two_parts(jnp.where(column == before, jnp.exp(cum[...]), 0.0))
    half = core if part == 0 else 1 - core
    offset = pl.multiple_of(half * HALF, HALF)
    carried = [
        jnp.dot(
            reads[...],
            state[:TOKENS, 256 * chunk : 256 * (chunk + 1)],
            preferred_element_type=f32,
        )
        for chunk in range(4)
    ]
    scale = [spread(factor, spread_matrix(chunk, offset)) for chunk in range(4)]
    copies = []
    for chunk in range(4):
        columns = pl.ds(pl.multiple_of(offset + 256 * chunk, 256), 256)
        local = slice(256 * chunk, 256 * (chunk + 1))
        result = inside[:, columns] + carried[chunk] * scale[chunk]
        held[:, local] = result.astype(bf16)
        copies += fetch([held.at[:, local]], [out.at[:, columns]], semaphores.at[pl.ds(chunk, 1)])
    for copy in copies:
        copy.wait()


def cut_kernel(keys, values, *refs):
    outs, semaphores = refs[:4], refs[4]
    x = lax.axis_index("tensor")
    sources, targets = [], []
    for step in range(4):
        columns = pl.ds(pl.multiple_of(((x + step) % 4) * DIM, DIM), DIM)
        sources += [keys.at[:, columns], values.at[:, columns]]
        targets += [outs[step].at[:, :DIM], outs[step].at[:, DIM:]]
    for copy in fetch(sources, targets, semaphores):
        copy.wait()


def assemble_kernel(p0, p1, p2, p3, docs, out):
    x = lax.axis_index("tensor")
    for step, ref in enumerate((p0, p1, p2, p3)):
        out[pl.ds(pl.multiple_of(((x - step) % 4) * 64, 64), 64), :] = ref[...]
    first = jnp.sum(jnp.where(docs[...] >= 1, 1.0, 0.0), axis=1, keepdims=True)
    second = jnp.sum(jnp.where(docs[...] >= 2, 1.0, 0.0), axis=1, keepdims=True)
    lane = iota(META, 2 * DIM, 1)
    counts = jnp.where(lane == 1, first, jnp.where(lane == 2, second, 0.0))
    out[TOKENS:] = jnp.where(lane == 0, float(TOKENS), counts).astype(bf16)


def chunk_kernel(mine, other, out):
    _, _, core = context_place()
    out[:ROWS] = jnp.where(core == 0, mine[...], other[...])
    out[ROWS:] = jnp.where(core == 0, other[...], mine[...])


def far_kernel(chunk, above, *outs):
    _, z, core = context_place()
    for step in range(1, 4):
        own = (core == 1) & ((z + step) % 4 > z)
        outs[step - 1][...] = jnp.where(own, chunk[...], above[...])


def bundle_kernel(a0, a1, a2, a3, out):
    for step, ref in enumerate((a0, a1, a2, a3)):
        out[2 * ROWS * step : 2 * ROWS * (step + 1)] = ref[...]


def chunk_of(blocks):
    one, two = blocks
    keys = jnp.concatenate([one[:, :DIM], two[:, :DIM]], axis=0)
    values = jnp.concatenate([one[:, DIM:], two[:, DIM:]], axis=0)
    values = jnp.concatenate([values.T, jnp.ones((META, CHUNK), bf16)], axis=0)
    return jnp.concatenate([keys, keys], axis=1), values


def mask_of(chunk, token, lowest):
    place = chunk * CHUNK + iota(CHUNK, TOKENS, 0)
    return jnp.where((place <= token) & (place >= lowest), 0.0, negative)


def fold(keys, values, bias, turned, peaks, sums, kind):
    def score(head):
        scores = jnp.dot(keys, turned[head], preferred_element_type=f32)
        return scores if bias is None else scores + bias

    def add(head, weights, shrink):
        new = jnp.dot(values, weights, preferred_element_type=f32)
        if kind == "first":
            sums[head] = new
        elif kind == "fixed":
            sums[head] = sums[head] + new
        else:
            sums[head] = sums[head] * shrink + new

    ahead = [score(head) for head in range(LEAD)]
    pending = None
    for head in range(REPEATS):
        if head + LEAD < REPEATS:
            ahead.append(score(head + LEAD))
        scores = ahead[head]
        shrink = None
        if kind == "fixed":
            new = peaks[head : head + 1]
        else:
            new = jnp.max(scores, axis=0, keepdims=True)
            if kind == "online":
                old = peaks[head : head + 1]
                new = jnp.maximum(old, new)
                shrink = jnp.exp2(old - new)
            peaks[head : head + 1] = new
        weights = jnp.exp2(scores - new).astype(bf16)
        if pending is not None:
            add(*pending)
        pending = (head, weights, shrink)
    add(*pending)


def starts_of(ids, start, base):
    below_one = jnp.sum(jnp.where(ids < 1, 1.0, 0.0)).astype(jnp.int32)
    below_two = jnp.sum(jnp.where(ids < 2, 1.0, 0.0)).astype(jnp.int32)
    opening = jnp.min(ids)
    return jnp.where(ids == opening, start, base + jnp.where(ids == 1, below_one, below_two))


def counted(counts, opening):
    here = (iota(META, 128, 0) == 0) & (iota(META, 128, 1) == opening)
    return jnp.sum(jnp.where(here, counts, 0.0)).astype(jnp.int32)


def own_kernel(queries, docs, chunk_ref, turned, peaks, sums):
    y, z, core = context_place()
    base = lax.axis_index("context") * TOKENS
    ids = docs[...]
    earlier = jnp.where(core == 1, chunk_ref[TOKENS:ROWS, :128].astype(f32), 0.0)
    lowest = starts_of(ids, base - counted(earlier, jnp.min(ids)), base)
    factor = math.log2(math.e) / math.sqrt(DIM)
    for head in range(REPEATS):
        scaled = (queries[:, head * DIM : (head + 1) * DIM].astype(f32) * factor).T
        high, middle, _ = split3(scaled)
        turned[head, :DIM] = high
        turned[head, DIM:] = middle
    bias = mask_of(y * 4 + z, base + iota(1, TOKENS, 1), lowest)
    keys, values = chunk_of([chunk_ref[:TOKENS], chunk_ref[ROWS : ROWS + TOKENS]])
    fold(keys, values, bias, turned, peaks, sums, "first")


def attention_kernel(docs, chunk_ref, bundle, arrived, turned, own_peaks, own_sums, out, peaks, sums):
    sums[...] = own_sums[...]
    y, z, core = context_place()
    base = lax.axis_index("context") * TOKENS
    own = y * 4 + z
    ids = docs[...]
    counts = jnp.where(core == 1, chunk_ref[TOKENS:ROWS, :128].astype(f32), 0.0)
    for block in range(8):
        rows = slice(block * ROWS + TOKENS, (block + 1) * ROWS)
        counts = counts + bundle[rows, :128].astype(f32) + arrived[rows, :128].astype(f32)
    start = base - counted(counts, jnp.min(ids))
    lowest = starts_of(ids, start, base)
    token = base + iota(1, TOKENS, 1)

    def visit(chunk, masked, peaks, kind):
        near = chunk // 4 == y - 1
        slot = ((z - chunk) % 4) * 2 * ROWS
        blocks = []
        for block in range(2):
            place = pl.ds(pl.multiple_of(slot + block * ROWS, ROWS), TOKENS)
            blocks.append(jnp.where(near == (core == 0), bundle[place, :], arrived[place, :]))
        keys, values = chunk_of(blocks)
        bias = mask_of(chunk, token, lowest) if masked else None
        fold(keys, values, bias, turned, peaks, sums, kind)

    first = start // CHUNK
    clear = jnp.minimum((jnp.max(lowest) + CHUNK - 1) // CHUNK, own)

    @pl.loop(first, clear)
    def _(chunk):
        visit(chunk, True, own_peaks, "fixed")

    @pl.loop(clear, own)
    def _(chunk):
        visit(chunk, False, own_peaks, "fixed")

    worst = jnp.max(jnp.concatenate([sums[head, DIM : DIM + 1] for head in range(REPEATS)], axis=0))

    @pl.when(jnp.logical_not(worst < 1e30))
    def _():
        peaks[...] = own_peaks[...]
        sums[...] = own_sums[...]

        @pl.loop(first, own)
        def _(chunk):
            visit(chunk, True, peaks, "online")

    for head in range(REPEATS):
        result = sums[head, :DIM] * (1.0 / sums[head, DIM : DIM + 1])
        out[:, head * DIM : (head + 1) * DIM] = result.T.astype(bf16)


def around_z(steps):
    return [
        (y * 8 + z * 2 + k, y * 8 + ((z + steps) % 4) * 2 + k)
        for y in range(4)
        for z in range(4)
        for k in range(2)
    ]


def along_y(steps):
    return [(c, c + 8 * steps) for c in range(BLOCKS - 8 * steps)]


def body(
    mixer_input,
    step_raw,
    step_bias,
    decay_log,
    skip_gain,
    write_keys,
    read_keys,
    document_ids,
    query_rows,
    key_rows,
    value_rows,
):
    docs = document_ids.reshape(1, TOKENS)
    across = [(c, c ^ 1) for c in range(BLOCKS)]
    below = [(c, c + 8 * (1 + c % 2)) for c in range(BLOCKS) if c + 8 * (1 + c % 2) < BLOCKS]

    cuts = run(
        cut_kernel,
        "cut_keys",
        [shape(64, 2 * DIM)] * 4,
        key_rows,
        value_rows,
        far=(0, 1),
        scratch=[pltpu.SemaphoreType.DMA((8,))],
        mib=56,
    )
    parts = [cuts[0]] + [
        lax.ppermute(cuts[step], "tensor", [(x, (x + step) % 4) for x in range(4)])
        for step in (1, 2, 3)
    ]

    mine, theirs, cum, offset = run(
        write_kernel,
        "mixer_write",
        [shape(ROWS, HALF), shape(ROWS, HALF), shape(TOKENS, HEADS, f32), shape(HEADS, TOKENS, f32)],
        step_raw.T,
        step_bias.reshape(1, HEADS),
        decay_log.reshape(1, HEADS),
        docs,
        mixer_input,
        write_keys,
        far=range(6),
        scratch=[
            pltpu.VMEM((HEADS, TOKENS), f32),
            pltpu.VMEM((1, HEADS), f32),
            pltpu.VMEM((1, HEADS), f32),
            pltpu.VMEM((1, TOKENS), jnp.int32),
            pltpu.VMEM((TOKENS, HEADS * WIDTH), bf16),
            pltpu.VMEM((TOKENS, DSTATE), bf16),
            pltpu.SemaphoreType.DMA((6,)),
        ],
        mib=56,
        flops=2 * 256 * 256 * 2048,
    )
    parts, mine, theirs, cum, offset = lax.optimization_barrier((parts, mine, theirs, cum, offset))
    (block,) = run(assemble_kernel, "assemble_keys", [shape(ROWS, 2 * DIM)], *parts, docs)
    other_block = lax.ppermute(block, "context", across)

    quarter = [shape(ROWS, QUARTER)]
    (chunk,) = run(chunk_kernel, "chunk_keys", [shape(2 * ROWS, 2 * DIM)], block, other_block)
    above = lax.ppermute(chunk, "context", below)
    theirs, chunk = lax.optimization_barrier((theirs, chunk))
    other = lax.ppermute(theirs, "context", across)
    chips = run(chip_kernel, "chip_state", quarter * 4, mine, other)
    slots = [chips[0]] + [lax.ppermute(chips[s], "context", around_z(s)) for s in (1, 2, 3)]

    (inside,) = run(
        inside_kernel,
        "mixer_inside",
        [shape(TOKENS, HEADS * WIDTH, f32)],
        cum,
        offset,
        docs,
        mixer_input,
        write_keys,
        read_keys,
        skip_gain.reshape(1, HEADS),
        mib=24,
        flops=2 * 256 * 256 * 128 * 32,
    )

    above, inside = lax.optimization_barrier((above, inside))
    far_cuts = run(far_kernel, "far_keys", [shape(2 * ROWS, 2 * DIM)] * 3, chunk, above)
    far = [lax.ppermute(far_cuts[s - 1], "context", around_z(s)) for s in (1, 2, 3)]

    slots, far_cuts = lax.optimization_barrier((slots, far_cuts))
    (row,) = run(row_kernel, "row_state", quarter, *slots)
    near_row = lax.ppermute(row, "context", along_y(1))
    far_row = lax.ppermute(row, "context", along_y(2))
    turned, peaks, sums = run(
        own_kernel,
        "attention_own",
        [
            jax.ShapeDtypeStruct((REPEATS, 2 * DIM, TOKENS), bf16),
            shape(REPEATS, TOKENS, f32),
            jax.ShapeDtypeStruct((REPEATS, DIM + META, TOKENS), f32),
        ],
        query_rows,
        docs,
        chunk,
        mib=24,
        flops=4 * 2048 * 512 * 128,
        transcendentals=2048 * 512,
    )
    near_row, far_row, turned = lax.optimization_barrier((near_row, far_row, turned))
    entering = run(entering_kernel, "entering_state", quarter * 4, *slots, near_row, far_row)
    back = [entering[0]] + [lax.ppermute(entering[s], "context", around_z(s)) for s in (1, 2, 3)]

    far, entering = lax.optimization_barrier((far, entering))
    (bundle,) = run(bundle_kernel, "bundle_keys", [shape(8 * ROWS, 2 * DIM)], above, *far)
    arrived = lax.ppermute(bundle, "context", across)

    (attended,) = run(
        attention_kernel,
        "attention",
        [shape(TOKENS, REPEATS * DIM)],
        docs,
        chunk,
        bundle,
        arrived,
        turned,
        peaks,
        sums,
        scratch=[
            pltpu.VMEM((REPEATS, TOKENS), f32),
            pltpu.VMEM((REPEATS, DIM + META, TOKENS), f32),
        ],
        mib=32,
        flops=4 * 2048 * 4096 * 128,
        transcendentals=2048 * 4096,
    )
    back, attended = lax.optimization_barrier((back, attended))

    keep, send = run(core_kernel, "core_state", [shape(ROWS, HALF)] * 2, *back, mine, other)
    state_arrived = lax.ppermute(send, "context", across)
    (own_half,) = run(
        functools.partial(carried_kernel, 0),
        "mixer_carried_own",
        [shape(TOKENS, HEADS * WIDTH)],
        inside,
        cum,
        docs,
        read_keys,
        keep,
        keep,
        onto=-1,
        scratch=[pltpu.VMEM((TOKENS, HALF), bf16), pltpu.SemaphoreType.DMA((4,))],
        mib=24,
        flops=2 * 256 * 256 * 1024,
    )
    state_arrived, own_half = lax.optimization_barrier((state_arrived, own_half))
    (mixed,) = run(
        functools.partial(carried_kernel, 1),
        "mixer_carried",
        [shape(TOKENS, HEADS * WIDTH)],
        inside,
        cum,
        docs,
        read_keys,
        keep,
        state_arrived,
        own_half,
        far=(6,),
        onto=6,
        scratch=[pltpu.VMEM((TOKENS, HALF), bf16), pltpu.SemaphoreType.DMA((4,))],
        mib=24,
        flops=2 * 256 * 256 * 1024,
    )
    return mixed, attended


def solution(mesh):
    placed = (
        P("context", "tensor"),
        P("context", "tensor"),
        P("tensor"),
        P("tensor"),
        P("tensor"),
        P("context", "tensor"),
        P("context", "tensor"),
        P("context"),
        P("context", "tensor"),
        P(("context", "tensor"), None),
        P(("context", "tensor"), None),
    )
    return jax.shard_map(
        body,
        mesh=mesh,
        in_specs=placed,
        out_specs=(P("context", "tensor"), P("context", "tensor")),
        check_vma=False,
    )
```
